256 devices in a mesh: rep: 16 (over x, y_hi, core), shard: 16 (over z, y_lo).
Axes of the slice: x: 4, y: 4 (y_hi: 2, y_lo: 2; y = y_hi * 2 + y_lo), z: 8, core: 2. Of those that a mesh axis runs over, the one named last changes fastest.
Arguments:
- tokens: bfloat16 [65536, 5120], P(('rep', 'shard')), may hold values from -12 to 12
- key_weight: bfloat16 [5120, 1024], P('shard'), may hold values from -0.2 to 0.2
- key_gain: float32 [1024], replicated, may hold values from 0.1 to 1.9
- key_cotangent: bfloat16 [65536, 1024], P(('rep', 'shard')), may hold values from -6 to 6
Outputs:
- grad_tokens: bfloat16 [65536, 5120], P(('rep', 'shard'))
- grad_weight: float32 [5120, 1024], P('shard')
- grad_gain: float32 [1024], replicated
The draws below stay inside these ranges and needn't reach their ends.
All inputs are finite; a program needn't handle non-finite values.
Results may differ from the reference program's by a relative error of at most 0.0049.
Values may be sent and summed in bfloat16 or wider, within the bound.
A program may use at most 128 MiB of HBM per device.

```python
import math
import jax
import jax.numpy as jnp
from jax import lax

D = 5120
KV = 1024
TOK_DEV = 256
TOKENS = 65536
N_REP = 16
N_SHARD = 16


def draw_tokens(key, part):
    key = jax.random.fold_in(key, 11)
    key_rows, key_values = jax.random.split(key, 2)
    scales = jnp.exp(jax.random.uniform(key_rows, (TOKENS, 1), jnp.float32, math.log(0.3), math.log(3.0)))
    values = jnp.clip(jax.random.normal(key_values, (TOKENS, D), jnp.float32), -4.0, 4.0)
    return (values * scales).astype(jnp.bfloat16)


def draw_key_weight(key, part):
    key = jax.random.fold_in(key, 23)
    key_cols, key_values = jax.random.split(key, 2)
    scales = jnp.exp(jax.random.uniform(key_cols, (1, KV), jnp.float32, math.log(0.3), math.log(3.0)))
    values = jnp.clip(jax.random.normal(key_values, (D, KV), jnp.float32), -4.0, 4.0)
    return (values * scales / math.sqrt(max(D, 5120))).astype(jnp.bfloat16)


def steps_of(stream_key, extent, shards, least, top_value):
    level = 1.0
    for dim, shards_of in shards:
        heights = jax.random.uniform(jax.random.fold_in(jax.random.fold_in(stream_key, 6), dim), (shards_of,), jnp.float32, least / len(shards), top_value / len(shards))
        level = level * jnp.repeat(jnp.exp(heights), extent[dim] // shards_of).reshape((-1,) + (1,) * (len(extent) - 1 - dim))
    return level


def normal_values(own_key, extent, scale, bound, pieces=(), held_as=jnp.bfloat16):
    result = jax.random.normal(own_key, extent, jnp.float32) * scale
    if len(pieces) > 0:
        result = steps_of(own_key, extent, pieces, -0.22, 0.18) * result
    return jnp.clip(result, min=-bound, max=bound).astype(held_as)


def setup_inputs(seed: int = 0) -> dict:
    seeds = jax.random.split(jax.random.key(seed), 5)
    tokens = draw_tokens(jax.random.fold_in(seeds[4], 71), 0)
    key_weight = draw_key_weight(jax.random.fold_in(seeds[4], 71), 0)
    key_gain = jnp.clip(1.0 + 0.18 * jax.random.normal(seeds[2], (KV,), jnp.float32), 0.1, 1.9)
    key_cotangent = normal_values(seeds[3], (TOKENS, KV), 1.0, 6.0, ((0, 256),))
    return dict(tokens=tokens, key_weight=key_weight, key_gain=key_gain, key_cotangent=key_cotangent)


def reference(tokens, key_weight, key_gain, key_cotangent):
    projected = jnp.dot(tokens, key_weight, preferred_element_type=jnp.float32)
    inverse = lax.rsqrt(lax.optimization_barrier(jnp.mean(projected * projected, axis=1, keepdims=True)) + 1e-06)
    normed = projected * inverse
    cotang = key_cotangent.astype(jnp.float32)
    scaled = cotang * key_gain
    dot_mean = lax.optimization_barrier(jnp.mean(scaled * normed, axis=1, keepdims=True))
    grad_keys = (inverse * (scaled - normed * dot_mean)).astype(jnp.bfloat16)
    grad_tokens = lax.dot_general(grad_keys, key_weight, (((1,), (1,)), ((), ())), preferred_element_type=jnp.float32).astype(jnp.bfloat16)
    devices = N_REP * N_SHARD
    token_blocks = tokens.reshape(devices, TOK_DEV, D)
    grad_blocks = grad_keys.reshape(devices, TOK_DEV, KV)

    def add_partial(summed, blocks):
        partial_value = lax.dot_general(blocks[0], blocks[1], (((0,), (0,)), ((), ())), preferred_element_type=jnp.float32)
        return (summed + partial_value, None)
    summed, unused = lax.scan(add_partial, jnp.zeros((D, KV), jnp.float32), (token_blocks, grad_blocks))
    grad_weight = summed / devices
    grad_gain = lax.optimization_barrier(jnp.sum(cotang * normed, axis=0)) / devices
    return (grad_tokens, grad_weight, grad_gain)
```

```python
import jax
import jax.numpy as jnp
from jax import lax
from jax.experimental import pallas as pl
from jax.experimental.pallas import tpu as pltpu
from jax.sharding import PartitionSpec as P

MESH = pl.DeviceIdType.MESH
F32 = jnp.float32
BF16 = jnp.bfloat16

ROWS = 320
PAIR = 640
COLS = 512
TOK = 256
CR = 192
CH = 96
AQ = 32
AH = 16
OFFS = (0, 1, -1, 2, -2, 3, -3, 4)
POS = {off: i for i, off in enumerate(OFFS)}
DEVICES = 256


def aligned(value, to):
    return pl.multiple_of(value, to)


def kernel(
    tok_ref, w_ref, gain_ref, cot_ref,
    gt_ref, gw_ref, gg_ref,
    W, X, COT, ACC, GK, ST, STR,
    G, XR, YR, ZR, SB, AX, TH, FO,
    TS, TR, TM, TO, GB, GR,
    lsem, *sems,
):
    rep, shard = lax.axis_index("rep"), lax.axis_index("shard")
    x, h, c = rep // 4, (rep // 2) % 2, rep % 2
    z, p = shard // 2, shard % 2
    y = 2 * h + p

    def dev(dx=0, dy=0, dz=0, core=None):
        xx, yy, zz = (x + dx) % 4, (y + dy) % 4, (z + dz) % 8
        cc = c if core is None else core
        return {"rep": xx * 4 + (yy // 2) * 2 + cc, "shard": zz * 2 + yy % 2}

    sibling = dev(core=1 - c)
    y_xor1 = dev(dy=1 - 2 * (y % 2))
    x_xor1 = dev(dx=1 - 2 * (x % 2))
    z_xor1 = dev(dz=1 - 2 * (z % 2))
    z_xor2 = dev(dz=2 - 4 * ((z // 2) % 2))
    z_xor4 = dev(dz=4)

    def zo(pos):
        return (z + OFFS[pos] + 8) % 8

    counters = {}
    open_sends = []

    def remote(group, src, dst, to):
        ss, rs = sems[2 * GROUPS.index(group)], sems[2 * GROUPS.index(group) + 1]
        i = counters.get(group, 0)
        counters[group] = i + 1
        assert i < SEMS[group], group
        return pltpu.make_async_remote_copy(
            src_ref=src, dst_ref=dst, send_sem=ss.at[i], recv_sem=rs.at[i],
            device_id=to, device_id_type=MESH,
        )

    def send(copy):
        copy.start()
        open_sends.append(copy)

    lcount = [0]

    def local(src, dst):
        i = lcount[0]
        lcount[0] += 1
        copy = pltpu.make_async_copy(src, dst, lsem.at[i])
        copy.start()
        return copy

    my_cols = pl.ds(aligned(c * COLS, COLS), COLS)
    sib_cols = pl.ds(aligned((1 - c) * COLS, COLS), COLS)
    my_toks = pl.ds(aligned(c * TOK, TOK), TOK)
    sib_toks = pl.ds(aligned((1 - c) * TOK, TOK), TOK)

    w_load = local(w_ref.at[:, my_cols], W.at[z, p])
    loads = [local(cot_ref.at[:, my_cols], COT.at[my_toks])]
    for q in range(8):
        loads.append(local(tok_ref.at[:, pl.ds(q * PAIR, PAIR)], X.at[q, my_toks]))

    partners = [dev(dx=1), dev(dx=2), dev(dx=3), dev(dy=1), dev(dy=2), dev(dy=3),
                dev(dz=1), dev(dz=7), z_xor2, z_xor4, sibling]
    barrier = pltpu.get_barrier_semaphore()
    for to in partners:
        pl.semaphore_signal(barrier, inc=1, device_id=to, device_id_type=MESH)
    pl.semaphore_wait(barrier, len(partners))

    crow = [pl.ds(k * CH, CH) for k in range(2)]
    arow = [pl.ds(aligned(CR + x * AQ + k * AH, AH), AH) for k in range(2)]
    axq = pl.ds(aligned(CR + x * AQ, AQ), AQ)
    zcp = {}
    ycp = {}
    xcp = {}

    def zsend(sig, d, k):
        at = zo(POS[-sig * (d - 1)] if d > 1 else 0)
        for part, rows in (("c", crow[k]), ("a", arow[k])):
            copy = remote("gz", W.at[at, p, rows], W.at[at, p, rows], dev(dz=sig % 8))
            zcp[sig, d, k, part] = copy
            send(copy)

    def zwait(sig, d, k):
        for part in ("c", "a"):
            zcp[sig, d, k, part].wait_recv()

    def ysend(pos, k):
        at = zo(pos)
        for part, rows in (("c", crow[k]), ("a", arow[k])):
            copy = remote("gy", W.at[at, p, rows], W.at[at, p, rows], dev(dy=1 if k == 0 else 3))
            ycp[pos, k, part] = copy
            send(copy)

    def ywait(pos):
        for k in range(2):
            for part in ("c", "a"):
                ycp[pos, k, part].wait_recv()

    def xsend(pos):
        at = zo(pos)
        for j in (1, 3, 2):
            if pos == 0:
                ref = W.at[at, pl.ds(1 - p, 1), axq]
            else:
                ref = W.at[at, :, axq]
            copy = remote("gx", ref, ref, dev(dx=j))
            xcp[pos, j] = copy
            send(copy)

    def xwait(pos):
        for j in (1, 3, 2):
            xcp[pos, j].wait_recv()

    def project(pos, first=False):
        at = zo(pos)

        @pl.loop(0, 2)
        def _(i):
            rows = pl.ds(aligned(i * TOK, TOK), TOK)
            part = jnp.dot(X[at, rows], W[at].reshape(PAIR, COLS), preferred_element_type=F32)
            if first:
                ACC[rows] = part
            else:
                ACC[rows] += part

    w_load.wait()
    zsend(1, 1, 0)
    zsend(-1, 1, 1)
    ysend(0, 0)
    ysend(0, 1)
    zsend(1, 1, 1)
    zsend(-1, 1, 0)
    swaps = [remote("swap", cot_ref.at[:, sib_cols], COT.at[my_toks], sibling)]
    for q in range(8):
        swaps.append(remote("swap", tok_ref.at[:, pl.ds(q * PAIR, PAIR)], X.at[q, my_toks], sibling))
    for copy in swaps:
        send(copy)

    def at_distance(d):
        return [0] if d == 0 else [7] if d == 4 else [POS[d], POS[-d]]

    for d in range(1, 7):
        if d <= 4:
            for j in range(2):
                for sig in (1, -1):
                    k = j if sig == 1 else 1 - j
                    if d == 4 and j == 1:
                        continue
                    zwait(sig, d, k)
                    if d < 3 or (d == 3 and j == 0):
                        zsend(sig, d + 1, k)
                    ysend(POS[-sig * d] if d < 4 else 7, k)
        if d - 1 <= 4:
            for pos in at_distance(d - 1):
                ywait(pos)
                xsend(pos)
        if d == 2:
            for copy in loads:
                copy.wait()
            for copy in swaps:
                copy.wait_recv()
        if d >= 2:
            for pos in at_distance(d - 2):
                xwait(pos)
                project(pos, first=pos == 0)

    gain = gain_ref[0:1, my_cols]

    @pl.loop(0, 4)
    def _(i):
        rows = pl.ds(aligned(i * 128, 128), 128)
        proj = ACC[rows]
        scaled = COT[rows].astype(F32) * gain
        ssq = jnp.sum(proj * proj, axis=1, keepdims=True)
        sdot = jnp.sum(scaled * proj, axis=1, keepdims=True)
        lane = lax.broadcasted_iota(jnp.int32, (128, 128), 1)
        ST[rows] = jnp.where(lane < 64, ssq, sdot)

    stats = remote("stat", ST, STR, sibling)
    stats.start()
    stats.wait()
    GB[0] = jnp.zeros((8, COLS), F32)

    @pl.loop(0, 4)
    def _(i):
        rows = pl.ds(aligned(i * 128, 128), 128)
        both = ST[rows] + STR[rows]
        ssq = both[:, 0:1] * (1.0 / (2 * COLS))
        sdot = both[:, 64:65] * (1.0 / (2 * COLS))
        inverse = lax.rsqrt(ssq + 1e-06)
        normed = ACC[rows] * inverse
        cot = COT[rows].astype(F32)
        scaled = cot * gain
        GK[rows] = (inverse * (scaled - normed * (inverse * sdot))).astype(BF16)
        GB[0] += jnp.broadcast_to(jnp.sum(cot * normed, axis=0, keepdims=True), (8, COLS))

    rxc, ryc, rza = {}, {}, {}
    other = 1 - p

    def s1(pos):
        at = zo(pos)
        G[at] = lax.dot_general(
            X[at], GK[...], (((0,), (0,)), ((), ())), preferred_element_type=F32
        ).astype(BF16).reshape(2, ROWS, COLS)
        for j in (1, 3, 2):
            rows = pl.ds(aligned(CR + ((x + j) % 4) * AQ, AQ), AQ)
            copy = remote("rx", G.at[at, :, rows], XR.at[pos, j - 1], dev(dx=j))
            rxc[pos, j] = copy
            send(copy)
        for k in range(2):
            copy = remote("ry", G.at[at, other, crow[k]], YR.at[pos, crow[k]], dev(dy=1 if k == 0 else 3))
            ryc[pos, k, "c"] = copy
            send(copy)

    def s2(pos):
        at = zo(pos)
        for j in (1, 3, 2):
            rxc[pos, j].wait_recv()
        for parity in range(2):
            total = G[at, parity, axq].astype(F32)
            for j in range(3):
                total = total + XR[pos, j, parity].astype(F32)
            G[at, parity, axq] = total.astype(BF16)
        for k in range(2):
            copy = remote("ry", G.at[at, other, arow[k]], YR.at[pos, pl.ds(CR + k * AH, AH)], dev(dy=1 if k == 0 else 3))
            ryc[pos, k, "a"] = copy
            send(copy)

    def s3(pos):
        for k in range(2):
            for part in ("c", "a"):
                ryc[pos, k, part].wait_recv()

    def halves_of(sig, d):
        return ([0] if sig == 1 else [1]) if d == 4 else ([0, 1] if sig == 1 else [1, 0])

    def s4(pos, sig):
        d = abs(OFFS[pos])
        at = zo(pos)
        for k in halves_of(sig, d):
            came = d < 3 or (d == 3 and k == (0 if sig == 1 else 1))
            for part, rows, buf in (("c", crow[k], crow[k]), ("a", arow[k], pl.ds(CR + k * AH, AH))):
                total = G[at, p, rows].astype(F32) + YR[pos, buf].astype(F32)
                if came:
                    rza[sig, d, k, part].wait_recv()
                    total = total + ZR[0 if sig == 1 else 1, d, buf].astype(F32)
                G[at, p, rows] = total.astype(BF16)
                copy = remote("rz", G.at[at, p, rows], ZR.at[0 if sig == 1 else 1, d - 1, buf], dev(dz=sig % 8))
                rza[sig, d - 1, k, part] = copy
                send(copy)

    gtc = {}
    outs = []

    def gt(pos):
        at = zo(pos)
        weight = W[at].reshape(PAIR, COLS)
        TS[pos] = lax.dot_general(
            GK[sib_toks], weight, (((1,), (1,)), ((), ())), preferred_element_type=F32
        ).astype(BF16)
        copy = remote("gt", TS.at[pos], TR.at[pos], sibling)
        gtc[pos] = copy
        send(copy)
        TM[pos] = lax.dot_general(
            GK[my_toks], weight, (((1,), (1,)), ((), ())), preferred_element_type=F32
        )

    def gt_end(pos):
        gtc[pos].wait_recv()
        TO[pos] = (TM[pos] + TR[pos].astype(F32)).astype(BF16)
        outs.append(local(TO.at[pos], gt_ref.at[:, pl.ds(aligned(zo(pos) * PAIR, 128), PAIR)]))

    gains = [x_xor1, dev(dx=2), y_xor1, dev(dy=2), z_xor1, z_xor2, z_xor4]
    ggc = {}

    def gain_send(i):
        ggc[i] = remote("gg", GB.at[i], GR.at[i], gains[i])
        send(ggc[i])

    def gain_add(i):
        ggc[i].wait_recv()
        GB[i + 1] = GB[i] + GR[i]

    def gain_step(i):
        gain_add(i)
        if i + 1 < len(gains):
            gain_send(i + 1)

    gain_send(0)
    s1(7)
    s1(5)
    s1(6)
    s2(7)
    s1(3)
    s1(4)
    s3(7)
    s4(7, 1)
    s4(7, -1)
    s2(5)
    s2(6)
    gain_step(0)
    s1(1)
    s1(2)
    s1(0)
    s3(5)
    s4(5, 1)
    s3(6)
    s4(6, -1)
    s2(3)
    s2(4)
    gain_step(1)
    gt(7)
    gt(5)
    gt(6)
    gt_end(7)
    s3(3)
    s4(3, 1)
    s3(4)
    s4(4, -1)
    s2(1)
    s2(2)
    gain_step(2)
    gt(3)
    gt(4)
    gt_end(5)
    gt_end(6)
    gain_step(3)
    s3(1)
    s4(1, 1)
    s3(2)
    s4(2, -1)
    s2(0)
    gain_step(4)
    gt(1)
    gt(2)
    gt(0)
    gt_end(3)
    gt_end(4)
    gain_step(5)
    gt_end(1)
    gt_end(2)
    gt_end(0)
    gain_step(6)
    GB[0 + 8] = GB[7] * (1.0 / DEVICES)
    gg_out = [local(GB.at[8], gg_ref.at[:, my_cols])]
    gg_far = remote("go", GB.at[8], gg_ref.at[:, my_cols], sibling)
    send(gg_far)

    s3(0)
    for sig in (1, -1):
        for k in halves_of(sig, 0):
            for part in ("c", "a"):
                rza[sig, 0, k, part].wait_recv()
    mine = YR[0, 0:CR].astype(F32) + G[z, p, 0:CR].astype(F32)
    mine = mine + ZR[0, 0, 0:CR].astype(F32) + ZR[1, 0, 0:CR].astype(F32)
    SB[...] = mine.astype(BF16)
    QC = CR // 4
    axc = {}
    for j in (1, 3, 2):
        rows = pl.ds(aligned(((x + j) % 4) * QC, 16), QC)
        axc[j] = remote("ax", SB.at[rows], AX.at[j - 1], dev(dx=j))
        send(axc[j])
    last = G[z, p, axq].astype(F32) + YR[0, CR:].astype(F32)
    TH[0, QC:] = last + ZR[0, 0, CR:].astype(F32) + ZR[1, 0, CR:].astype(F32)
    for j in (1, 3, 2):
        axc[j].wait_recv()
    total = SB[pl.ds(aligned(x * QC, 16), QC)].astype(F32)
    for j in range(3):
        total = total + AX[j].astype(F32)
    TH[0, 0:QC] = total
    swap_h = remote("ah", TH.at[0], TH.at[1], dev(dy=2))
    send(swap_h)
    swap_h.wait_recv()
    crows = pl.ds(aligned(x * QC, 16), QC)
    FO[crows] = (TH[0, 0:QC] + TH[1, 0:QC]) * (1.0 / DEVICES)
    FO[axq] = (TH[0, QC:] + TH[1, QC:]) * (1.0 / DEVICES)
    fin = []
    for j in (1, 3, 2):
        for rows in (crows, axq):
            copy = remote("af", FO.at[rows], FO.at[rows], dev(dx=j))
            fin.append(copy)
            send(copy)
    for copy in fin:
        copy.wait_recv()
    gw_out = local(FO, gw_ref.at[:, my_cols])
    gw_far = remote("go", FO, gw_ref.at[:, my_cols], sibling)
    send(gw_far)
    gw_far.wait_recv()
    gg_far.wait_recv()
    gw_out.wait()
    for copy in gg_out + outs:
        copy.wait()
    for copy in open_sends:
        copy.wait_send()


SEMS = {"gz": 28, "gy": 32, "gx": 24, "swap": 9, "stat": 1, "rx": 24, "ry": 32, "rz": 28, "gt": 8, "gg": 7,
        "go": 2, "ax": 3, "ah": 1, "af": 6}
GROUPS = tuple(SEMS)


def per_device(tokens, key_weight, key_gain, key_cotangent):
    anywhere = pl.BlockSpec(memory_space=pl.ANY)
    vmem = pl.BlockSpec(memory_space=pltpu.VMEM)
    sems = []
    for group in GROUPS:
        sems += [pltpu.SemaphoreType.DMA((SEMS[group],))] * 2
    V = pltpu.VMEM
    grad_tokens, grad_weight, grad_gain = pl.pallas_call(
        kernel,
        out_shape=(
            jax.ShapeDtypeStruct((TOK, 5120), BF16),
            jax.ShapeDtypeStruct((ROWS, 1024), F32),
            jax.ShapeDtypeStruct((8, 1024), F32),
        ),
        in_specs=[anywhere, anywhere, vmem, anywhere],
        out_specs=(anywhere, anywhere, anywhere),
        scratch_shapes=[
            V((8, 2, ROWS, COLS), BF16),
            V((8, 2 * TOK, PAIR), BF16),
            V((2 * TOK, COLS), BF16),
            V((2 * TOK, COLS), F32),
            V((2 * TOK, COLS), BF16),
            V((2 * TOK, 128), F32),
            V((2 * TOK, 128), F32),
            V((8, 2, ROWS, COLS), BF16),
            V((8, 3, 2, AQ, COLS), BF16),
            V((8, CR + AQ, COLS), BF16),
            V((2, 4, CR + AQ, COLS), BF16),
            V((CR, COLS), BF16),
            V((3, CR // 4, COLS), BF16),
            V((2, ROWS // 4, COLS), F32),
            V((ROWS, COLS), F32),
            V((8, TOK, PAIR), BF16),
            V((8, TOK, PAIR), BF16),
            V((8, TOK, PAIR), F32),
            V((8, TOK, PAIR), BF16),
            V((9, 8, COLS), F32),
            V((7, 8, COLS), F32),
            pltpu.SemaphoreType.DMA((24,)),
            *sems,
        ],
        compiler_params=pltpu.CompilerParams(
            collective_id=0, has_side_effects=True, vmem_limit_bytes=60 * 2**20
        ),
        name="key_projection_backward",
    )(tokens, key_weight, key_gain.reshape(1, 1024), key_cotangent)
    return grad_tokens, grad_weight, grad_gain[0]


def solution(mesh):
    return jax.shard_map(
        per_device,
        mesh=mesh,
        in_specs=(P(("rep", "shard"), None), P("shard", None), P(), P(("rep", "shard"), None)),
        out_specs=(P(("rep", "shard"), None), P("shard", None), P()),
        check_vma=False,
    )
```

```python
import jax
import jax.numpy as jnp
from jax import lax
from jax.experimental import pallas as pl
from jax.experimental.pallas import tpu as pltpu
from jax.sharding import PartitionSpec as P

MESH = pl.DeviceIdType.MESH
F32 = jnp.float32
BF16 = jnp.bfloat16

ROWS = 320
PAIR = 640
COLS = 512
TOK = 256
CR = 192
CH = 96
AQ = 32
AH = 16
OFFS = (0, 1, -1, 2, -2, 3, -3, 4)
POS = {off: i for i, off in enumerate(OFFS)}
DEVICES = 256
THT = F32


def aligned(value, to):
    return pl.multiple_of(value, to)


def kernel(
    tok_ref, w_ref, gain_ref, cot_ref,
    gt_ref, gw_ref, gg_ref,
    W, X, COT, ACC, GK, ST, STR,
    G, XR, YR, ZR, SB, AX, TH, FO,
    TS, TR, TM, TO, GB, GX, GY, GZ,
    lsem, *sems,
):
    rep, shard = lax.axis_index("rep"), lax.axis_index("shard")
    x, h, c = rep // 4, (rep // 2) % 2, rep % 2
    z, p = shard // 2, shard % 2
    y = 2 * h + p

    def dev(dx=0, dy=0, dz=0, core=None):
        xx, yy, zz = (x + dx) % 4, (y + dy) % 4, (z + dz) % 8
        cc = c if core is None else core
        return {"rep": xx * 4 + (yy // 2) * 2 + cc, "shard": zz * 2 + yy % 2}

    sibling = dev(core=1 - c)
    def zo(pos):
        return (z + OFFS[pos] + 8) % 8

    counters = {}
    open_sends = []

    def remote(group, src, dst, to):
        ss, rs = sems[2 * GROUPS.index(group)], sems[2 * GROUPS.index(group) + 1]
        i = counters.get(group, 0)
        counters[group] = i + 1
        assert i < SEMS[group], group
        return pltpu.make_async_remote_copy(
            src_ref=src, dst_ref=dst, send_sem=ss.at[i], recv_sem=rs.at[i],
            device_id=to, device_id_type=MESH,
        )

    def send(copy):
        copy.start()
        open_sends.append(copy)

    lcount = [0]

    def local(src, dst):
        i = lcount[0]
        lcount[0] += 1
        copy = pltpu.make_async_copy(src, dst, lsem.at[i])
        copy.start()
        return copy

    my_cols = pl.ds(aligned(c * COLS, COLS), COLS)
    sib_cols = pl.ds(aligned((1 - c) * COLS, COLS), COLS)
    my_toks = pl.ds(aligned(c * TOK, TOK), TOK)
    sib_toks = pl.ds(aligned((1 - c) * TOK, TOK), TOK)

    w_load = local(w_ref.at[:, my_cols], W.at[z, p])
    loads = [local(cot_ref.at[:, my_cols], COT.at[my_toks])]
    for q in range(8):
        loads.append(local(tok_ref.at[:, pl.ds(q * PAIR, PAIR)], X.at[q, my_toks]))

    partners = [dev(dx=i) for i in range(1, 4)] + [dev(dy=i) for i in range(1, 4)]
    partners += [dev(dz=i) for i in range(1, 8)] + [sibling]
    barrier = pltpu.get_barrier_semaphore()
    for to in partners:
        pl.semaphore_signal(barrier, inc=1, device_id=to, device_id_type=MESH)
    pl.semaphore_wait(barrier, len(partners))

    crow = [pl.ds(k * CH, CH) for k in range(2)]
    arow = [pl.ds(aligned(CR + x * AQ + k * AH, AH), AH) for k in range(2)]
    axq = pl.ds(aligned(CR + x * AQ, AQ), AQ)
    cp = {}

    def at_step(sig, d):
        return 0 if d == 0 else 7 if d == 4 else POS[-sig * d]

    def zc(sig, d, k):
        ref = W.at[zo(at_step(sig, d - 1)), p, crow[k]]
        cp["zc", sig, d, k] = remote("gz", ref, ref, dev(dz=sig % 8))
        send(cp["zc", sig, d, k])

    def za(sig, d):
        rows = axq if d < 4 else arow[0 if sig == 1 else 1]
        ref = W.at[zo(at_step(sig, d - 1)), p, rows]
        cp["za", sig, d] = remote("gz", ref, ref, dev(dz=sig % 8))
        send(cp["za", sig, d])

    def yc(pos, k):
        ref = W.at[zo(pos), p, crow[k]]
        cp["yc", pos, k] = remote("gy", ref, ref, dev(dy=1 if k == 0 else 3))
        send(cp["yc", pos, k])

    def ya(pos, k):
        ref = W.at[zo(pos), p, arow[k]]
        cp["ya", pos, k] = remote("gy", ref, ref, dev(dy=1 if k == 0 else 3))
        send(cp["ya", pos, k])

    def xs(pos):
        for j in (1, 3, 2):
            ref = W.at[zo(pos), pl.ds(1 - p, 1), axq] if pos == 0 else W.at[zo(pos), :, axq]
            cp["x", pos, j] = remote("gx", ref, ref, dev(dx=j))
            send(cp["x", pos, j])

    def got(*key):
        cp[key].wait_recv()

    def project(pos, first=False):
        at = zo(pos)

        @pl.loop(0, 2)
        def _(i):
            rows = pl.ds(aligned(i * TOK, TOK), TOK)
            part = jnp.dot(X[at, rows], W[at].reshape(PAIR, COLS), preferred_element_type=F32)
            if first:
                ACC[rows] = part
            else:
                ACC[rows] += part

    def positions(d):
        return [0] if d == 0 else [7] if d == 4 else [POS[d], POS[-d]]

    def a_step(d):
        for sig in (1, -1):
            got("za", sig, d)
            if d < 4:
                za(sig, d + 1)
                for k in range(2):
                    ya(at_step(sig, d), k)
            else:
                ya(7, 0 if sig == 1 else 1)

    def ax_step(d):
        for pos in positions(d):
            for k in range(2):
                got("ya", pos, k)
            xs(pos)

    def c_step(d, j):
        for sig in (1, -1):
            k = j if sig == 1 else 1 - j
            got("zc", sig, d, k)
            if d < 3 or (d == 3 and j == 0):
                zc(sig, d + 1, k)
            yc(at_step(sig, d), k)

    def finish(d):
        for pos in positions(d):
            for k in range(2):
                got("yc", pos, k)
            for j in (1, 3, 2):
                got("x", pos, j)
            project(pos, first=pos == 0)

    w_load.wait()
    za(1, 1)
    za(-1, 1)
    ya(0, 0)
    ya(0, 1)
    zc(1, 1, 0)
    zc(-1, 1, 1)
    yc(0, 0)
    yc(0, 1)
    swaps = [remote("swap", cot_ref.at[:, sib_cols], COT.at[my_toks], sibling)]
    for q in range(8):
        swaps.append(remote("swap", tok_ref.at[:, pl.ds(q * PAIR, PAIR)], X.at[q, my_toks], sibling))
    for copy in swaps:
        send(copy)
    a_step(1)
    zc(1, 1, 1)
    zc(-1, 1, 0)
    ax_step(0)
    c_step(1, 0)
    a_step(2)
    ax_step(1)
    c_step(1, 1)
    a_step(3)
    ax_step(2)
    a_step(4)
    c_step(2, 0)
    ax_step(3)
    c_step(2, 1)
    ax_step(4)
    for copy in loads:
        copy.wait()
    for copy in swaps:
        copy.wait_recv()
    c_step(3, 0)
    finish(0)
    c_step(3, 1)
    finish(1)
    c_step(4, 0)
    finish(2)
    finish(3)
    finish(4)

    gain = gain_ref[0:1, my_cols]

    @pl.loop(0, 4)
    def _(i):
        rows = pl.ds(aligned(i * 128, 128), 128)
        proj = ACC[rows]
        scaled = COT[rows].astype(F32) * gain
        ssq = jnp.sum(proj * proj, axis=1, keepdims=True)
        sdot = jnp.sum(scaled * proj, axis=1, keepdims=True)
        lane = lax.broadcasted_iota(jnp.int32, (128, 128), 1)
        ST[rows] = jnp.where(lane < 64, ssq, sdot)

    stats = remote("stat", ST, STR, sibling)
    stats.start()
    stats.wait()
    GX[x] = jnp.zeros((8, COLS), F32)

    @pl.loop(0, 4)
    def _(i):
        rows = pl.ds(aligned(i * 128, 128), 128)
        both = ST[rows] + STR[rows]
        ssq = both[:, 0:1] * (1.0 / (2 * COLS))
        sdot = both[:, 64:65] * (1.0 / (2 * COLS))
        inverse = lax.rsqrt(ssq + 1e-06)
        normed = ACC[rows] * inverse
        cot = COT[rows].astype(F32)
        scaled = cot * gain
        GK[rows] = (inverse * (scaled - normed * (inverse * sdot))).astype(BF16)
        GX[x] += jnp.broadcast_to(jnp.sum(cot * normed, axis=0, keepdims=True), (8, COLS))

    other = 1 - p
    half = [pl.ds(CR + k * AH, AH) for k in range(2)]

    def half_of(quarter, k):
        return pl.ds(aligned(CR + (quarter % 4) * AQ + k * AH, AH), AH)

    def partial(pos):
        G[zo(pos)] = lax.dot_general(
            X[zo(pos)], GK[...], (((0,), (0,)), ((), ())), preferred_element_type=F32
        ).astype(BF16).reshape(2, ROWS, COLS)

    def y_wide(pos):
        for k in range(2):
            cp["yw", pos, k] = remote("ry", G.at[zo(pos), other, crow[k]], YR.at[pos, crow[k]], dev(dy=1 if k == 0 else 3))
            send(cp["yw", pos, k])

    def x_first(pos):
        at = zo(pos)
        for way in range(2):
            step = 1 if way == 0 else 3
            rows = half_of(x + 2, way)
            cp["x1", pos, way] = remote("rx", G.at[at, :, rows], XR.at[pos, way, 0], dev(dx=step))
            send(cp["x1", pos, way])
            rows = half_of(x + step, 1 - way)
            cp["x2", pos, way] = remote("rx", G.at[at, :, rows], XR.at[pos, way, 1], dev(dx=step))
            send(cp["x2", pos, way])

    def x_second(pos):
        at = zo(pos)
        for way in range(2):
            step = 1 if way == 0 else 3
            rows = half_of(x + step, way)
            got("x1", pos, way)
            for parity in range(2):
                G[at, parity, rows] = (G[at, parity, rows].astype(F32) + XR[pos, way, 0, parity].astype(F32)).astype(BF16)
            cp["x3", pos, way] = remote("rx", G.at[at, :, rows], XR.at[pos, way, 2], dev(dx=step))
            send(cp["x3", pos, way])

    def x_third(pos):
        at = zo(pos)
        for way in range(2):
            got("x2", pos, way)
            got("x3", pos, way)
        for k in range(2):
            for parity in range(2):
                total = G[at, parity, arow[k]].astype(F32) + XR[pos, k, 2, parity].astype(F32)
                total = total + XR[pos, 1 - k, 1, parity].astype(F32)
                G[at, parity, arow[k]] = total.astype(BF16)
        for k in range(2):
            cp["yn", pos, k] = remote("ry", G.at[at, other, arow[k]], YR.at[pos, half[k]], dev(dy=1 if k == 0 else 3))
            send(cp["yn", pos, k])

    def owner(sig, d):
        return 0 if d == 0 else 7 if d == 4 else POS[sig * d]

    def first_half(sig):
        return 0 if sig == 1 else 1

    def z_sum(sig, d, k, rows, buf, name):
        pos, at, way = owner(sig, d), zo(owner(sig, d)), 0 if sig == 1 else 1
        got("y" + name, pos, k)
        total = G[at, p, rows].astype(F32) + YR[pos, buf].astype(F32)
        if d < 3 or (d == 3 and k == first_half(sig)):
            got("z" + name, sig, d, k)
            total = total + ZR[way, d, buf].astype(F32)
        G[at, p, rows] = total.astype(BF16)
        cp["z" + name, sig, d - 1, k] = remote("rz", G.at[at, p, rows], ZR.at[way, d - 1, buf], dev(dz=sig % 8))
        send(cp["z" + name, sig, d - 1, k])

    def z_wide(d, j):
        for sig in (1, -1):
            k = first_half(sig) if j == 1 else 1 - first_half(sig)
            z_sum(sig, d, k, crow[k], crow[k], "w")

    def z_narrow(d):
        for sig in (1, -1):
            for k in ([first_half(sig)] if d == 4 else [1 - first_half(sig), first_half(sig)]):
                z_sum(sig, d, k, arow[k], half[k], "n")

    gtc = {}
    outs = []

    def gt(pos):
        at = zo(pos)
        weight = W[at].reshape(PAIR, COLS)
        TS[pos] = lax.dot_general(
            GK[sib_toks], weight, (((1,), (1,)), ((), ())), preferred_element_type=F32
        ).astype(BF16)
        copy = remote("gt", TS.at[pos], TR.at[pos], sibling)
        gtc[pos] = copy
        send(copy)
        TM[pos] = lax.dot_general(
            GK[my_toks], weight, (((1,), (1,)), ((), ())), preferred_element_type=F32
        )

    def gt_end(pos):
        gtc[pos].wait_recv()
        TO[pos] = (TM[pos] + TR[pos].astype(F32)).astype(BF16)
        outs.append(local(TO.at[pos], gt_ref.at[:, pl.ds(aligned(zo(pos) * PAIR, 128), PAIR)]))

    def gain_send(name, buf, mine, hops):
        for hop in hops:
            cp["gain" + name, hop] = remote("gg", buf.at[mine], buf.at[mine], dev(**{"d" + name: hop}))
            send(cp["gain" + name, hop])

    def gain_sum(name, buf, hops):
        for hop in hops:
            got("gain" + name, hop)
        total = buf[0]
        for i in range(1, len(hops) + 1):
            total = total + buf[i]
        return total

    def gain_step(i):
        if i == 0:
            gain_send("x", GX, x, (1, 3, 2))
        elif i == 1:
            GY[y] = gain_sum("x", GX, (1, 3, 2))
            gain_send("y", GY, y, (1, 3, 2))
        elif i == 2:
            GZ[z] = gain_sum("y", GY, (1, 3, 2))
            gain_send("z", GZ, z, (1, 7, 2, 6, 3, 5, 4))
        else:
            GB[...] = gain_sum("z", GZ, (1, 7, 2, 6, 3, 5, 4)) * (1.0 / DEVICES)

    gain_step(0)
    partial(7)
    y_wide(7)
    x_first(7)
    partial(5)
    y_wide(5)
    partial(6)
    y_wide(6)
    x_first(5)
    x_first(6)
    partial(3)
    y_wide(3)
    partial(4)
    y_wide(4)
    z_wide(4, 1)
    x_second(7)
    partial(1)
    y_wide(1)
    z_wide(3, 0)
    x_first(3)
    partial(2)
    y_wide(2)
    x_second(5)
    x_third(7)
    x_first(4)
    partial(0)
    y_wide(0)
    z_wide(3, 1)
    x_second(6)
    x_third(5)
    x_first(1)
    z_wide(2, 0)
    x_second(3)
    x_third(6)
    z_narrow(4)
    x_first(2)
    gt(7)
    gain_step(1)
    z_wide(2, 1)
    x_second(4)
    x_third(3)
    x_first(0)
    gt(5)
    z_wide(1, 0)
    x_second(1)
    x_third(4)
    z_narrow(3)
    gt(6)
    gain_step(2)
    z_wide(1, 1)
    x_second(2)
    x_third(1)
    gt(3)
    z_narrow(2)
    x_second(0)
    x_third(2)
    gt(4)
    z_narrow(1)
    x_third(0)
    gt(1)
    gt(2)
    gt(0)
    QC = CR // 4
    for sig in (1, -1):
        for k in range(2):
            got("zw", sig, 0, k)
    for k in range(2):
        got("yw", 0, k)
    mine = YR[0, 0:CR].astype(F32) + G[z, p, 0:CR].astype(F32)
    mine = mine + ZR[0, 0, 0:CR].astype(F32) + ZR[1, 0, 0:CR].astype(F32)
    SB[...] = mine.astype(BF16)
    for j in (1, 3, 2):
        rows = pl.ds(aligned(((x + j) % 4) * QC, 16), QC)
        cp["ax", j] = remote("ax", SB.at[rows], AX.at[j - 1], dev(dx=j))
        send(cp["ax", j])
    for sig in (1, -1):
        for k in range(2):
            got("zn", sig, 0, k)
    for k in range(2):
        got("yn", 0, k)
    last = G[z, p, axq].astype(F32) + YR[0, CR:].astype(F32)
    TH[0, QC:] = (last + ZR[0, 0, CR:].astype(F32) + ZR[1, 0, CR:].astype(F32)).astype(TH.dtype)
    ah = [remote("ah", TH.at[0, pl.ds(QC, AQ)], TH.at[1, pl.ds(QC, AQ)], dev(dy=2))]
    send(ah[0])
    for q in (7, 5, 6, 3, 4, 1, 2, 0):
        gt_end(q)
    gain_step(3)
    gg_out = [local(GB, gg_ref.at[:, my_cols])]
    gg_far = remote("go", GB, gg_ref.at[:, my_cols], sibling)
    send(gg_far)

    for j in (1, 3, 2):
        got("ax", j)
    crows = pl.ds(aligned(x * QC, 16), QC)
    total = SB[crows].astype(F32)
    for j in range(3):
        total = total + AX[j].astype(F32)
    TH[0, 0:QC] = total.astype(TH.dtype)
    ah.append(remote("ah", TH.at[0, pl.ds(0, QC)], TH.at[1, pl.ds(0, QC)], dev(dy=2)))
    send(ah[1])
    fin = {}
    for i, rows, buf in ((0, axq, pl.ds(QC, AQ)), (1, crows, pl.ds(0, QC))):
        ah[i].wait_recv()
        FO[c, rows] = ((TH[0, buf].astype(F32) + TH[1, buf].astype(F32)) * (1.0 / DEVICES)).astype(BF16)
        for j in (1, 3, 2):
            fin[i, j] = remote("af", FO.at[c, rows], FO.at[c, rows], dev(dx=j))
            send(fin[i, j])
        fin[i, 0] = remote("ac", FO.at[c, rows], FO.at[c, rows], sibling)
        send(fin[i, 0])
    far = []
    for j in (1, 3, 2):
        source = (x + 4 - j) % 4
        for i, rows in ((0, pl.ds(aligned(CR + source * AQ, AQ), AQ)), (1, pl.ds(aligned(source * QC, 16), QC))):
            fin[i, j].wait_recv()
            copy = remote("ac", FO.at[c, rows], FO.at[c, rows], sibling)
            far.append(copy)
            send(copy)
    for copy in far + [fin[0, 0], fin[1, 0]]:
        copy.wait_recv()
    gw_out = local(FO, gw_ref)
    gg_far.wait_recv()
    gw_out.wait()
    for copy in gg_out + outs:
        copy.wait()
    for copy in open_sends:
        copy.wait_send()


def finish(gt_in, gw_in, gg_in, gt_ref, gw_ref, gg_ref, buf, sem):
    parts = [pl.ds(i * TOK // 4, TOK // 4) for i in range(4)]
    reads = [pltpu.make_async_copy(gt_in.at[rows], buf.at[rows], sem.at[0, i]) for i, rows in enumerate(parts)]
    writes = [pltpu.make_async_copy(buf.at[rows], gt_ref.at[rows], sem.at[1, i]) for i, rows in enumerate(parts)]
    for read in reads:
        read.start()
    for half in range(2):
        gw_ref[:, half * COLS : (half + 1) * COLS] = gw_in[half].astype(F32)
    gg_ref[...] = gg_in[0:1]
    for read, write in zip(reads, writes):
        read.wait()
        write.start()
    for write in writes:
        write.wait()


SEMS = {"gz": 30, "gy": 32, "gx": 24, "swap": 9, "stat": 1, "rx": 48, "ry": 32, "rz": 28, "gt": 8, "gg": 13,
        "go": 1, "ax": 3, "ah": 2, "af": 6, "ac": 8}
GROUPS = tuple(SEMS)


def per_device(tokens, key_weight, key_gain, key_cotangent):
    anywhere = pl.BlockSpec(memory_space=pl.ANY)
    vmem = pl.BlockSpec(memory_space=pltpu.VMEM)
    sems = []
    for group in GROUPS:
        sems += [pltpu.SemaphoreType.DMA((SEMS[group],))] * 2
    V = pltpu.VMEM
    grad_tokens, grad_weight, grad_gain = pl.pallas_call(
        kernel,
        out_shape=(
            jax.ShapeDtypeStruct((TOK, 5120), BF16),
            jax.ShapeDtypeStruct((2, ROWS, COLS), BF16),
            jax.ShapeDtypeStruct((8, 1024), F32),
        ),
        in_specs=[anywhere, anywhere, vmem, anywhere],
        out_specs=(anywhere, anywhere, anywhere),
        scratch_shapes=[
            V((8, 2, ROWS, COLS), BF16),
            V((8, 2 * TOK, PAIR), BF16),
            V((2 * TOK, COLS), BF16),
            V((2 * TOK, COLS), F32),
            V((2 * TOK, COLS), BF16),
            V((2 * TOK, 128), F32),
            V((2 * TOK, 128), F32),
            V((8, 2, ROWS, COLS), BF16),
            V((8, 2, 3, 2, AH, COLS), BF16),
            V((8, CR + AQ, COLS), BF16),
            V((2, 4, CR + AQ, COLS), BF16),
            V((CR, COLS), BF16),
            V((3, CR // 4, COLS), BF16),
            V((2, ROWS // 4, COLS), THT),
            V((2, ROWS, COLS), BF16),
            V((8, TOK, PAIR), BF16),
            V((8, TOK, PAIR), BF16),
            V((8, TOK, PAIR), F32),
            V((8, TOK, PAIR), BF16),
            V((8, COLS), F32),
            V((4, 8, COLS), F32),
            V((4, 8, COLS), F32),
            V((8, 8, COLS), F32),
            pltpu.SemaphoreType.DMA((24,)),
            *sems,
        ],
        compiler_params=pltpu.CompilerParams(
            collective_id=0, has_side_effects=True, vmem_limit_bytes=60 * 2**20
        ),
        name="key_projection_backward",
    )(tokens, key_weight, key_gain.reshape(1, 1024), key_cotangent)
    grad_tokens, grad_weight, grad_gain = pl.pallas_call(
        finish,
        out_shape=(
            jax.ShapeDtypeStruct((TOK, 5120), BF16),
            jax.ShapeDtypeStruct((ROWS, 1024), F32),
            jax.ShapeDtypeStruct((1, 1024), F32),
        ),
        in_specs=[anywhere, vmem, vmem],
        out_specs=(anywhere, vmem, vmem),
        scratch_shapes=[pltpu.VMEM((TOK, 5120), BF16), pltpu.SemaphoreType.DMA((2, 4))],
        name="write_results",
    )(grad_tokens, grad_weight, grad_gain)
    return grad_tokens, grad_weight, grad_gain.reshape(1024)


def solution(mesh):
    return jax.shard_map(
        per_device,
        mesh=mesh,
        in_specs=(P(("rep", "shard"), None), P("shard", None), P(), P(("rep", "shard"), None)),
        out_specs=(P(("rep", "shard"), None), P("shard", None), P()),
        check_vma=False,
    )
```

```python
import jax
import jax.numpy as jnp
from jax import lax
from jax.experimental import pallas as pl
from jax.experimental.pallas import tpu as pltpu
from jax.sharding import PartitionSpec as P

MESH = pl.DeviceIdType.MESH
F32 = jnp.float32
BF16 = jnp.bfloat16

ROWS = 320
PAIR = 640
COLS = 512
TOK = 256
CR = 192
CH = 96
AQ = 32
AH = 16
OFFS = (0, 1, -1, 2, -2, 3, -3, 4)
POS = {off: i for i, off in enumerate(OFFS)}
DEVICES = 256


def aligned(value, to):
    return pl.multiple_of(value, to)


def kernel(
    tok_ref, w_ref, gain_ref, cot_ref,
    gt_ref, gw_ref, gg_ref,
    W, X, COT, ACC, GK, ST, STR,
    G, XR, YR, ZR, SB, SF, AX, NB, NR, FO,
    TS, TR, TM, GB, GX, GY, GZ,
    lsem, *sems,
):
    rep, shard = lax.axis_index("rep"), lax.axis_index("shard")
    x, h, c = rep // 4, (rep // 2) % 2, rep % 2
    z, p = shard // 2, shard % 2
    y = 2 * h + p

    def dev(dx=0, dy=0, dz=0, core=None):
        xx, yy, zz = (x + dx + 4) % 4, (y + dy) % 4, (z + dz) % 8
        cc = c if core is None else core
        return {"rep": xx * 4 + (yy // 2) * 2 + cc, "shard": zz * 2 + yy % 2}

    sibling = dev(core=1 - c)
    def zo(pos):
        return (z + OFFS[pos] + 8) % 8

    counters = {}
    open_sends = []

    def remote(group, src, dst, to):
        ss, rs = sems[2 * GROUPS.index(group)], sems[2 * GROUPS.index(group) + 1]
        i = counters.get(group, 0)
        counters[group] = i + 1
        assert i < SEMS[group], group
        return pltpu.make_async_remote_copy(
            src_ref=src, dst_ref=dst, send_sem=ss.at[i], recv_sem=rs.at[i],
            device_id=to, device_id_type=MESH,
        )

    def send(copy):
        copy.start()
        open_sends.append(copy)

    lcount = [0]

    def local(src, dst):
        i = lcount[0]
        lcount[0] += 1
        copy = pltpu.make_async_copy(src, dst, lsem.at[i])
        copy.start()
        return copy

    my_cols = pl.ds(aligned(c * COLS, COLS), COLS)
    sib_cols = pl.ds(aligned((1 - c) * COLS, COLS), COLS)
    my_toks = pl.ds(aligned(c * TOK, TOK), TOK)
    sib_toks = pl.ds(aligned((1 - c) * TOK, TOK), TOK)

    w_load = local(w_ref.at[:, my_cols], W.at[z, p])
    loads = [local(cot_ref.at[:, my_cols], COT.at[my_toks])]
    for q in range(8):
        loads.append(local(tok_ref.at[:, pl.ds(q * PAIR, PAIR)], X.at[q, my_toks]))

    partners = [dev(dx=i) for i in range(1, 4)] + [dev(dy=i) for i in range(1, 4)]
    partners += [dev(dz=i) for i in range(1, 8)] + [dev(dx=i, dy=2) for i in range(1, 4)] + [sibling]
    barrier = pltpu.get_barrier_semaphore()
    for to in partners:
        pl.semaphore_signal(barrier, inc=1, device_id=to, device_id_type=MESH)
    pl.semaphore_wait(barrier, len(partners))

    crow = [pl.ds(k * CH, CH) for k in range(2)]
    arow = [pl.ds(aligned(CR + x * AQ + k * AH, AH), AH) for k in range(2)]
    axq = pl.ds(aligned(CR + x * AQ, AQ), AQ)
    cp, seen = {}, set()

    def at_step(sig, d):
        return 0 if d == 0 else 7 if d == 4 else POS[-sig * d]

    def zc(sig, d, k):
        ref = W.at[zo(at_step(sig, d - 1)), p, crow[k]]
        cp["zc", sig, d, k] = remote("gz", ref, ref, dev(dz=sig % 8))
        send(cp["zc", sig, d, k])

    def za(sig, d):
        rows = axq if d < 4 else arow[0 if sig == 1 else 1]
        ref = W.at[zo(at_step(sig, d - 1)), p, rows]
        cp["za", sig, d] = remote("gz", ref, ref, dev(dz=sig % 8))
        send(cp["za", sig, d])

    def yc(pos, k):
        ref = W.at[zo(pos), p, crow[k]]
        cp["yc", pos, k] = remote("gy", ref, ref, dev(dy=1 if k == 0 else 3))
        send(cp["yc", pos, k])

    def ya(pos, k):
        ref = W.at[zo(pos), p, arow[k]]
        cp["ya", pos, k] = remote("gy", ref, ref, dev(dy=1 if k == 0 else 3))
        send(cp["ya", pos, k])

    def half_of(quarter, k):
        return pl.ds(aligned(CR + (quarter % 4) * AQ + k * AH, AH), AH)

    def xs(pos):
        for k in range(2):
            got("ya", pos, k)
        ref = W.at[zo(pos), pl.ds(1 - p, 1), axq] if pos == 0 else W.at[zo(pos), :, axq]
        for way in range(2):
            cp["xs", pos, way] = remote("gx", ref, ref, dev(dx=1 if way == 0 else 3))
            send(cp["xs", pos, way])

    def xr(pos, way):
        got("xs", pos, way)
        rows = half_of(x + (3 if way == 0 else 1), way)
        ref = W.at[zo(pos), pl.ds(1 - p, 1), rows] if pos == 0 else W.at[zo(pos), :, rows]
        cp["xr", pos, way] = remote("gx", ref, ref, dev(dx=1 if way == 0 else 3))
        send(cp["xr", pos, way])

    def got(*key):
        if key not in seen:
            seen.add(key)
            cp[key].wait_recv()

    def project(pos, first=False):
        at = zo(pos)

        @pl.loop(0, 2)
        def _(i):
            rows = pl.ds(aligned(i * TOK, TOK), TOK)
            part = jnp.dot(X[at, rows], W[at].reshape(PAIR, COLS), preferred_element_type=F32)
            if first:
                ACC[rows] = part
            else:
                ACC[rows] += part

    def positions(d):
        return [0] if d == 0 else [7] if d == 4 else [POS[d], POS[-d]]

    def a_step(d):
        for sig in (1, -1):
            got("za", sig, d)
            if d < 4:
                za(sig, d + 1)
                for k in range(2):
                    ya(at_step(sig, d), k)
            else:
                ya(7, 0 if sig == 1 else 1)

    def ax_step(d):
        for pos in positions(d):
            xs(pos)

    def xr_step(d):
        for pos in positions(d):
            xr(pos, 0)
            xr(pos, 1)

    def c_step(d, j):
        for sig in (1, -1):
            k = j if sig == 1 else 1 - j
            got("zc", sig, d, k)
            if d < 3 or (d == 3 and j == 0):
                zc(sig, d + 1, k)
            yc(at_step(sig, d), k)

    def finish(d):
        for pos in positions(d):
            for k in range(2):
                got("yc", pos, k)
            for way in range(2):
                got("xs", pos, way)
                got("xr", pos, way)
            project(pos, first=pos == 0)

    w_load.wait()
    za(1, 1)
    za(-1, 1)
    ya(0, 0)
    ya(0, 1)
    zc(1, 1, 0)
    zc(-1, 1, 1)
    yc(0, 0)
    yc(0, 1)
    swaps = [remote("swap", cot_ref.at[:, sib_cols], COT.at[my_toks], sibling)]
    for q in range(8):
        swaps.append(remote("swap", tok_ref.at[:, pl.ds(q * PAIR, PAIR)], X.at[q, my_toks], sibling))
    for copy in swaps:
        send(copy)
    a_step(1)
    zc(1, 1, 1)
    zc(-1, 1, 0)
    ax_step(0)
    c_step(1, 0)
    a_step(2)
    ax_step(1)
    c_step(1, 1)
    a_step(3)
    c_step(2, 0)
    ax_step(2)
    xr_step(0)
    a_step(4)
    c_step(2, 1)
    xr_step(1)
    ax_step(3)
    ax_step(4)
    c_step(3, 0)
    xr_step(2)
    for copy in loads:
        copy.wait()
    for copy in swaps:
        copy.wait_recv()
    finish(0)
    c_step(3, 1)
    xr_step(3)
    c_step(4, 0)
    xr_step(4)
    finish(1)
    finish(2)
    finish(3)
    finish(4)

    gain = gain_ref[0:1, my_cols]

    lane = lax.broadcasted_iota(jnp.int32, (128, 128), 1)
    stats = []
    for i in range(4):
        rows = pl.ds(i * 128, 128)
        proj = ACC[rows]
        scaled = COT[rows].astype(F32) * gain
        ssq = jnp.sum(proj * proj, axis=1, keepdims=True)
        sdot = jnp.sum(scaled * proj, axis=1, keepdims=True)
        ST[rows] = jnp.where(lane < 64, ssq, sdot)
        stats.append(remote("stat", ST.at[rows], STR.at[rows], sibling))
        send(stats[i])
    gain_part = jnp.zeros((1, COLS), F32)
    for i in range(4):
        rows = pl.ds(i * 128, 128)
        stats[i].wait_recv()
        both = ST[rows] + STR[rows]
        ssq = both[:, 0:1] * (1.0 / (2 * COLS))
        sdot = both[:, 64:65] * (1.0 / (2 * COLS))
        inverse = lax.rsqrt(ssq + 1e-06)
        normed = ACC[rows] * inverse
        cot = COT[rows].astype(F32)
        scaled = cot * gain
        GK[rows] = (inverse * (scaled - normed * (inverse * sdot))).astype(BF16)
        gain_part += jnp.sum(cot * normed, axis=0, keepdims=True)
    GX[x] = gain_part

    other = 1 - p
    half = [pl.ds(CR + k * AH, AH) for k in range(2)]

    def partial(pos):
        G[zo(pos)] = lax.dot_general(
            X[zo(pos)], GK[...], (((0,), (0,)), ((), ())), preferred_element_type=F32
        ).astype(BF16).reshape(2, ROWS, COLS)

    def y_wide(pos):
        for k in range(2):
            cp["yw", pos, k] = remote("ry", G.at[zo(pos), other, crow[k]], YR.at[pos, crow[k]], dev(dy=1 if k == 0 else 3))
            send(cp["yw", pos, k])

    def x_far(pos):
        for way in range(2):
            rows = half_of(x + 2, way)
            cp["x1", pos, way] = remote("rx", G.at[zo(pos), :, rows], XR.at[pos, way, 0], dev(dx=1 if way == 0 else 3))
            send(cp["x1", pos, way])

    def x_near(pos):
        for way in range(2):
            step = 1 if way == 0 else 3
            rows = half_of(x + step, 1 - way)
            cp["x2", pos, way] = remote("rx", G.at[zo(pos), :, rows], XR.at[pos, way, 1], dev(dx=step))
            send(cp["x2", pos, way])

    def x_second(pos, way):
        at = zo(pos)
        step = 1 if way == 0 else 3
        rows = half_of(x + step, way)
        got("x1", pos, way)
        for parity in range(2):
            G[at, parity, rows] = (G[at, parity, rows].astype(F32) + XR[pos, way, 0, parity].astype(F32)).astype(BF16)
        cp["x3", pos, way] = remote("rx", G.at[at, :, rows], XR.at[pos, way, 2], dev(dx=step))
        send(cp["x3", pos, way])

    def x_third(pos):
        at = zo(pos)
        for way in range(2):
            got("x2", pos, way)
            got("x3", pos, way)
        for k in range(2):
            for parity in range(2):
                total = G[at, parity, arow[k]].astype(F32) + XR[pos, k, 2, parity].astype(F32)
                total = total + XR[pos, 1 - k, 1, parity].astype(F32)
                G[at, parity, arow[k]] = total.astype(BF16)
        for k in range(2):
            cp["yn", pos, k] = remote("ry", G.at[at, other, arow[k]], YR.at[pos, half[k]], dev(dy=1 if k == 0 else 3))
            send(cp["yn", pos, k])

    def owner(sig, d):
        return 0 if d == 0 else 7 if d == 4 else POS[sig * d]

    def first_half(sig):
        return 0 if sig == 1 else 1

    def z_sum(sig, d, k, name):
        pos, at, way = owner(sig, d), zo(owner(sig, d)), 0 if sig == 1 else 1
        rows, buf = (crow[k], crow[k]) if name == "w" else (arow[k], half[k])
        got("y" + name, pos, k)
        total = G[at, p, rows].astype(F32) + YR[pos, buf].astype(F32)
        if d < 3 or (d == 3 and k == first_half(sig)):
            got("z" + name, sig, d, k)
            total = total + ZR[way, d, buf].astype(F32)
        G[at, p, rows] = total.astype(BF16)
        cp["z" + name, sig, d - 1, k] = remote("rz", G.at[at, p, rows], ZR.at[way, d - 1, buf], dev(dz=sig % 8))
        send(cp["z" + name, sig, d - 1, k])

    gtc = {}

    def gt(pos):
        at = zo(pos)
        weight = W[at].reshape(PAIR, COLS)
        TS[pos] = lax.dot_general(
            GK[sib_toks], weight, (((1,), (1,)), ((), ())), preferred_element_type=F32
        ).astype(BF16)
        copy = remote("gt", TS.at[pos], TR.at[pos], sibling)
        gtc[pos] = copy
        send(copy)
        TM[pos] = lax.dot_general(
            GK[my_toks], weight, (((1,), (1,)), ((), ())), preferred_element_type=F32
        )

    def gt_end(pos):
        gtc[pos].wait_recv()
        gt_ref[:, pl.ds(aligned(zo(pos) * PAIR, 128), PAIR)] = (TM[pos] + TR[pos].astype(F32)).astype(BF16)

    def gain_send(name, buf, mine, hops):
        for hop in hops:
            cp["gain" + name, hop] = remote("gg", buf.at[mine], buf.at[mine], dev(**{"d" + name: hop}))
            send(cp["gain" + name, hop])

    def gain_sum(name, buf, hops):
        for hop in hops:
            got("gain" + name, hop)
        total = buf[0]
        for i in range(1, len(hops) + 1):
            total = total + buf[i]
        return total

    def gain_step(i):
        if i == 0:
            gain_send("x", GX, x, (1, 3, 2))
        elif i == 1:
            GY[y] = gain_sum("x", GX, (1, 3, 2))
            gain_send("y", GY, y, (1, 3, 2))
        elif i == 2:
            GZ[z] = gain_sum("y", GY, (1, 3, 2))
            gain_send("z", GZ, z, (1, 7, 2, 6, 3, 5, 4))
        else:
            GB[...] = gain_sum("z", GZ, (1, 7, 2, 6, 3, 5, 4)) * (1.0 / DEVICES)

    gain_step(0)
    partial(7)
    x_far(7)
    y_wide(7)
    partial(5)
    x_near(7)
    partial(6)
    x_far(5)
    partial(3)
    x_near(5)
    y_wide(5)
    partial(4)
    x_second(7, 0)
    x_second(7, 1)
    partial(1)
    partial(2)
    x_far(6)
    partial(0)
    x_near(6)
    z_sum(-1, 4, 1, 'w')
    y_wide(6)
    z_sum(1, 4, 0, 'w')
    x_far(3)
    x_second(5, 1)
    x_second(5, 0)
    gt(7)
    x_third(7)
    gt(5)
    x_near(3)
    y_wide(3)
    z_sum(1, 3, 1, 'w')
    x_second(6, 0)
    x_second(6, 1)
    gt(6)
    x_far(4)
    x_second(3, 0)
    x_second(3, 1)
    gt(3)
    z_sum(-1, 3, 1, 'w')
    gain_step(1)
    z_sum(1, 4, 0, 'n')
    z_sum(-1, 4, 1, 'n')
    y_wide(4)
    x_near(4)
    z_sum(1, 3, 0, 'w')
    z_sum(-1, 3, 0, 'w')
    x_third(5)
    x_far(1)
    x_third(6)
    gt(4)
    x_near(1)
    x_second(4, 0)
    z_sum(1, 2, 1, 'w')
    x_second(4, 1)
    x_third(3)
    gt(1)
    x_far(2)
    y_wide(1)
    gt(2)
    x_near(2)
    x_second(1, 1)
    z_sum(-1, 2, 1, 'w')
    z_sum(1, 2, 0, 'w')
    z_sum(1, 3, 1, 'n')
    z_sum(1, 3, 0, 'n')
    x_second(1, 0)
    z_sum(-1, 3, 1, 'n')
    z_sum(-1, 3, 0, 'n')
    x_third(4)
    x_far(0)
    gain_step(2)
    gt(0)
    x_near(0)
    z_sum(-1, 2, 0, 'w')
    y_wide(2)
    x_second(2, 0)
    x_second(2, 1)
    x_third(1)
    z_sum(1, 1, 1, 'w')
    x_second(0, 0)
    x_second(0, 1)
    y_wide(0)
    z_sum(1, 1, 0, 'w')
    z_sum(-1, 2, 1, 'n')
    z_sum(1, 2, 1, 'n')
    z_sum(-1, 2, 0, 'n')
    z_sum(1, 2, 0, 'n')
    x_third(2)
    z_sum(-1, 1, 1, 'w')
    x_third(0)
    z_sum(-1, 1, 0, 'w')
    z_sum(-1, 1, 0, 'n')
    z_sum(-1, 1, 1, 'n')
    z_sum(1, 1, 1, 'n')
    z_sum(1, 1, 0, 'n')

    others = [(1, 0), (3, 0), (2, 0), (0, 1), (1, 1), (3, 1), (2, 1)]

    def wide_block(dx, dh):
        return pl.ds(aligned((h + dh) % 2 * CH, CH), CH), pl.ds(aligned((x + dx + 4) % 4 * 128, 128), 128)

    def narrow_block(dx, dh):
        return pl.ds(aligned(CR + (x + dx + 4) % 4 * AQ + (h + dh) % 2 * AH, AH), AH)

    for sig in (1, -1):
        for k in range(2):
            got("zw", sig, 0, k)
    for k in range(2):
        got("yw", 0, k)
    mine = YR[0, 0:CR].astype(F32) + G[z, p, 0:CR].astype(F32)
    mine = mine + ZR[0, 0, 0:CR].astype(F32) + ZR[1, 0, 0:CR].astype(F32)
    SF[...] = mine
    SB[...] = mine.astype(BF16)
    for i, (dx, dh) in enumerate(others):
        cp["ax", i] = remote("ax", SB.at[wide_block(dx, dh)], AX.at[i], dev(dx=dx, dy=2 * dh))
        send(cp["ax", i])
    for sig in (1, -1):
        for k in range(2):
            got("zn", sig, 0, k)
    for k in range(2):
        got("yn", 0, k)
    last = G[z, p, axq].astype(F32) + YR[0, CR:].astype(F32)
    NB[...] = last + ZR[0, 0, CR:].astype(F32) + ZR[1, 0, CR:].astype(F32)
    ah = remote("ah", NB.at[pl.ds(aligned((1 - h) * AH, AH), AH)], NR, dev(dy=2))
    send(ah)
    for q in (7, 5, 6, 3, 4, 1, 2, 0):
        gt_end(q)
    def hand_out(name, ref):
        for i, (dx, dh) in enumerate(others):
            cp[name, i] = remote("af", ref, ref, dev(dx=dx, dy=2 * dh))
            send(cp[name, i])
        far.append(remote("ac", ref, ref, sibling))
        send(far[-1])

    far = []
    ah.wait_recv()
    FO[c, narrow_block(0, 0)] = ((NB[pl.ds(aligned(h * AH, AH), AH)] + NR[...]) * (1.0 / DEVICES)).astype(BF16)
    hand_out("narrow", FO.at[c, narrow_block(0, 0)])
    total = SF[wide_block(0, 0)]
    for i in range(len(others)):
        got("ax", i)
        total = total + AX[i].astype(F32)
    FO[(c,) + wide_block(0, 0)] = (total * (1.0 / DEVICES)).astype(BF16)
    hand_out("wide", FO.at[(c,) + wide_block(0, 0)])
    gain_step(3)
    gg_out = [local(GB, gg_ref.at[:, my_cols])]
    gg_far = remote("go", GB, gg_ref.at[:, my_cols], sibling)
    send(gg_far)

    for i, (dx, dh) in enumerate(others):
        for name, ref in (("narrow", FO.at[c, narrow_block(-dx, dh)]), ("wide", FO.at[(c,) + wide_block(-dx, dh)])):
            got(name, i)
            far.append(remote("ac", ref, ref, sibling))
            send(far[-1])
    for copy in far:
        copy.wait_recv()
    gw_ref[...] = FO[...]
    gg_far.wait_recv()
    for copy in gg_out:
        copy.wait()
    for copy in open_sends:
        copy.wait_send()


def finish(gt_in, gw_in, gg_in, gt_ref, gw_ref, gg_ref, wide, sem):
    copies = []
    for i in range(4):
        rows = pl.ds(i * TOK // 4, TOK // 4)
        copies.append(pltpu.make_async_copy(gt_in.at[rows], gt_ref.at[rows], sem.at[i]))
    copies.append(pltpu.make_async_copy(gg_in, gg_ref, sem.at[4]))
    for copy in copies:
        copy.start()
    for i in range(2):
        rows = pl.ds(i * ROWS // 2, ROWS // 2)
        for half in range(2):
            wide[rows, half * COLS : (half + 1) * COLS] = gw_in[half, rows].astype(F32)
        copies.append(pltpu.make_async_copy(wide.at[rows], gw_ref.at[rows], sem.at[5 + i]))
        copies[-1].start()
    for copy in copies:
        copy.wait()


SEMS = {"gz": 30, "gy": 32, "gx": 32, "swap": 9, "stat": 4, "rx": 48, "ry": 32, "rz": 28, "gt": 8, "gg": 13,
        "go": 1, "ax": 7, "ah": 1, "af": 14, "ac": 16}
GROUPS = tuple(SEMS)


def per_device(tokens, key_weight, key_gain, key_cotangent):
    anywhere = pl.BlockSpec(memory_space=pl.ANY)
    vmem = pl.BlockSpec(memory_space=pltpu.VMEM)
    sems = []
    for group in GROUPS:
        sems += [pltpu.SemaphoreType.DMA((SEMS[group],))] * 2
    V = pltpu.VMEM
    grad_tokens, grad_weight, grad_gain = pl.pallas_call(
        kernel,
        out_shape=(
            pltpu.VMEM((TOK, 5120), BF16),
            pltpu.VMEM((2, ROWS, COLS), BF16),
            pltpu.VMEM((1, 1024), F32),
        ),
        in_specs=[anywhere, anywhere, vmem, anywhere],
        out_specs=(vmem, vmem, vmem),
        scratch_shapes=[
            V((8, 2, ROWS, COLS), BF16),
            V((8, 2 * TOK, PAIR), BF16),
            V((2 * TOK, COLS), BF16),
            V((2 * TOK, COLS), F32),
            V((2 * TOK, COLS), BF16),
            V((2 * TOK, 128), F32),
            V((2 * TOK, 128), F32),
            V((8, 2, ROWS, COLS), BF16),
            V((8, 2, 3, 2, AH, COLS), BF16),
            V((8, CR + AQ, COLS), BF16),
            V((2, 4, CR + AQ, COLS), BF16),
            V((CR, COLS), BF16),
            V((CR, COLS), F32),
            V((7, CH, 128), BF16),
            V((AQ, COLS), F32),
            V((AH, COLS), F32),
            V((2, ROWS, COLS), BF16),
            V((8, TOK, PAIR), BF16),
            V((8, TOK, PAIR), BF16),
            V((8, TOK, PAIR), F32),
            V((1, COLS), F32),
            V((4, 1, COLS), F32),
            V((4, 1, COLS), F32),
            V((8, 1, COLS), F32),
            pltpu.SemaphoreType.DMA((24,)),
            *sems,
        ],
        compiler_params=pltpu.CompilerParams(
            collective_id=0, has_side_effects=True, vmem_limit_bytes=58 * 2**20
        ),
        name="key_projection_backward",
    )(tokens, key_weight, key_gain.reshape(1, 1024), key_cotangent)
    grad_tokens, grad_weight, grad_gain = pl.pallas_call(
        finish,
        out_shape=(
            jax.ShapeDtypeStruct((TOK, 5120), BF16),
            jax.ShapeDtypeStruct((ROWS, 1024), F32),
            jax.ShapeDtypeStruct((1, 1024), F32),
        ),
        in_specs=[vmem, vmem, vmem],
        out_specs=(anywhere, anywhere, anywhere),
        scratch_shapes=[pltpu.VMEM((ROWS, 1024), F32), pltpu.SemaphoreType.DMA((7,))],
        compiler_params=pltpu.CompilerParams(vmem_limit_bytes=16 * 2**20),
        name="write_results",
    )(grad_tokens, grad_weight, grad_gain)
    return grad_tokens, grad_weight, grad_gain.reshape(1024)


def solution(mesh):
    return jax.shard_map(
        per_device,
        mesh=mesh,
        in_specs=(P(("rep", "shard"), None), P("shard", None), P(), P(("rep", "shard"), None)),
        out_specs=(P(("rep", "shard"), None), P("shard", None), P()),
        check_vma=False,
    )
```

```python
import jax
import jax.numpy as jnp
from jax import lax
from jax.experimental import pallas as pl
from jax.experimental.pallas import tpu as pltpu
from jax.sharding import PartitionSpec as P

MESH = pl.DeviceIdType.MESH
F32 = jnp.float32
BF16 = jnp.bfloat16

ROWS = 320
PAIR = 640
COLS = 512
TOK = 256
CR = 192
CH = 96
AQ = 32
AH = 16
OFFS = (0, 1, -1, 2, -2, 3, -3, 4)
POS = {off: i for i, off in enumerate(OFFS)}
DEVICES = 256


def aligned(value, to):
    return pl.multiple_of(value, to)


def kernel(
    tok_ref, w_ref, gain_ref, cot_ref,
    gt_ref, gw_ref, gg_ref,
    W, X, COT, ACC, GK, ST, STR,
    G, XR, YR, ZR, SB, SF, AX, NB, NR, FO,
    TS, TR, TM, GB, GX, GY, GZ,
    lsem, *sems,
):
    rep, shard = lax.axis_index("rep"), lax.axis_index("shard")
    x, h, c = rep // 4, (rep // 2) % 2, rep % 2
    z, p = shard // 2, shard % 2
    y = 2 * h + p

    def dev(dx=0, dy=0, dz=0, core=None):
        xx, yy, zz = (x + dx + 4) % 4, (y + dy) % 4, (z + dz) % 8
        cc = c if core is None else core
        return {"rep": xx * 4 + (yy // 2) * 2 + cc, "shard": zz * 2 + yy % 2}

    sibling = dev(core=1 - c)
    def zo(pos):
        return (z + OFFS[pos] + 8) % 8

    counters = {}
    open_sends = []

    def remote(group, src, dst, to):
        ss, rs = sems[2 * GROUPS.index(group)], sems[2 * GROUPS.index(group) + 1]
        i = counters.get(group, 0)
        counters[group] = i + 1
        assert i < SEMS[group], group
        return pltpu.make_async_remote_copy(
            src_ref=src, dst_ref=dst, send_sem=ss.at[i], recv_sem=rs.at[i],
            device_id=to, device_id_type=MESH,
        )

    def send(copy):
        copy.start()
        open_sends.append(copy)

    lcount = [0]

    def local(src, dst):
        i = lcount[0]
        lcount[0] += 1
        copy = pltpu.make_async_copy(src, dst, lsem.at[i])
        copy.start()
        return copy

    my_cols = pl.ds(aligned(c * COLS, COLS), COLS)
    sib_cols = pl.ds(aligned((1 - c) * COLS, COLS), COLS)
    my_toks = pl.ds(aligned(c * TOK, TOK), TOK)
    sib_toks = pl.ds(aligned((1 - c) * TOK, TOK), TOK)

    w_load = local(w_ref.at[:, my_cols], W.at[z, p])
    loads = [local(cot_ref.at[:, my_cols], COT.at[my_toks])]
    for q in range(8):
        loads.append(local(tok_ref.at[:, pl.ds(q * PAIR, PAIR)], X.at[q, my_toks]))

    partners = [dev(dx=i) for i in range(1, 4)] + [dev(dy=i) for i in range(1, 4)]
    partners += [dev(dz=i) for i in range(1, 8)] + [dev(dx=i, dy=2) for i in range(1, 4)] + [sibling]
    barrier = pltpu.get_barrier_semaphore()
    for to in partners:
        pl.semaphore_signal(barrier, inc=1, device_id=to, device_id_type=MESH)
    pl.semaphore_wait(barrier, len(partners))

    crow = [pl.ds(k * CH, CH) for k in range(2)]
    arow = [pl.ds(aligned(CR + x * AQ + k * AH, AH), AH) for k in range(2)]
    axq = pl.ds(aligned(CR + x * AQ, AQ), AQ)
    cp, seen = {}, set()

    def at_step(sig, d):
        return 0 if d == 0 else 7 if d == 4 else POS[-sig * d]

    def zc(sig, d, k):
        ref = W.at[zo(at_step(sig, d - 1)), p, crow[k]]
        cp["zc", sig, d, k] = remote("gz", ref, ref, dev(dz=sig % 8))
        send(cp["zc", sig, d, k])

    def za(sig, d):
        rows = axq if d < 4 else arow[0 if sig == 1 else 1]
        ref = W.at[zo(at_step(sig, d - 1)), p, rows]
        cp["za", sig, d] = remote("gz", ref, ref, dev(dz=sig % 8))
        send(cp["za", sig, d])

    def yc(pos, k):
        ref = W.at[zo(pos), p, crow[k]]
        cp["yc", pos, k] = remote("gy", ref, ref, dev(dy=1 if k == 0 else 3))
        send(cp["yc", pos, k])

    def ya(pos, k):
        ref = W.at[zo(pos), p, arow[k]]
        cp["ya", pos, k] = remote("gy", ref, ref, dev(dy=1 if k == 0 else 3))
        send(cp["ya", pos, k])

    def half_of(quarter, k):
        return pl.ds(aligned(CR + (quarter % 4) * AQ + k * AH, AH), AH)

    def xs(pos):
        for k in range(2):
            got("ya", pos, k)
        ref = W.at[zo(pos), pl.ds(1 - p, 1), axq] if pos == 0 else W.at[zo(pos), :, axq]
        for way in range(2):
            cp["xs", pos, way] = remote("gx", ref, ref, dev(dx=1 if way == 0 else 3))
            send(cp["xs", pos, way])

    def xr(pos, way):
        got("xs", pos, way)
        rows = half_of(x + (3 if way == 0 else 1), way)
        ref = W.at[zo(pos), pl.ds(1 - p, 1), rows] if pos == 0 else W.at[zo(pos), :, rows]
        cp["xr", pos, way] = remote("gx", ref, ref, dev(dx=1 if way == 0 else 3))
        send(cp["xr", pos, way])

    def got(*key):
        if key not in seen:
            seen.add(key)
            cp[key].wait_recv()

    def project(pos, first=False):
        at = zo(pos)

        @pl.loop(0, 2)
        def _(i):
            rows = pl.ds(aligned(i * TOK, TOK), TOK)
            part = jnp.dot(X[at, rows], W[at].reshape(PAIR, COLS), preferred_element_type=F32)
            if first:
                ACC[rows] = part
            else:
                ACC[rows] += part

    def positions(d):
        return [0] if d == 0 else [7] if d == 4 else [POS[d], POS[-d]]

    def a_step(d):
        for sig in (1, -1):
            got("za", sig, d)
            if d < 4:
                za(sig, d + 1)
                for k in range(2):
                    ya(at_step(sig, d), k)
            else:
                ya(7, 0 if sig == 1 else 1)

    def ax_step(d):
        for pos in positions(d):
            xs(pos)

    def xr_step(d):
        for pos in positions(d):
            xr(pos, 0)
            xr(pos, 1)

    def c_step(d, j):
        for sig in (1, -1):
            k = j if sig == 1 else 1 - j
            got("zc", sig, d, k)
            if d < 3 or (d == 3 and j == 0):
                zc(sig, d + 1, k)
            yc(at_step(sig, d), k)

    def finish(d):
        for pos in positions(d):
            for k in range(2):
                got("yc", pos, k)
            for way in range(2):
                got("xs", pos, way)
                got("xr", pos, way)
            project(pos, first=pos == 0)

    w_load.wait()
    za(1, 1)
    za(-1, 1)
    ya(0, 0)
    ya(0, 1)
    zc(1, 1, 0)
    zc(-1, 1, 1)
    yc(0, 0)
    yc(0, 1)
    swaps = [remote("swap", cot_ref.at[:, sib_cols], COT.at[my_toks], sibling)]
    for q in range(8):
        swaps.append(remote("swap", tok_ref.at[:, pl.ds(q * PAIR, PAIR)], X.at[q, my_toks], sibling))
    for copy in swaps:
        send(copy)
    a_step(1)
    zc(1, 1, 1)
    zc(-1, 1, 0)
    ax_step(0)
    c_step(1, 0)
    a_step(2)
    ax_step(1)
    c_step(1, 1)
    a_step(3)
    c_step(2, 0)
    ax_step(2)
    xr_step(0)
    a_step(4)
    c_step(2, 1)
    xr_step(1)
    ax_step(3)
    ax_step(4)
    c_step(3, 0)
    xr_step(2)
    for copy in loads:
        copy.wait()
    for copy in swaps:
        copy.wait_recv()
    finish(0)
    c_step(3, 1)
    xr_step(3)
    c_step(4, 0)
    xr_step(4)
    finish(1)
    finish(2)
    finish(3)
    finish(4)

    gain = gain_ref[0:1, my_cols]

    lane = lax.broadcasted_iota(jnp.int32, (128, 128), 1)
    stats = []
    for i in range(4):
        rows = pl.ds(i * 128, 128)
        proj = ACC[rows]
        scaled = COT[rows].astype(F32) * gain
        ssq = jnp.sum(proj * proj, axis=1, keepdims=True)
        sdot = jnp.sum(scaled * proj, axis=1, keepdims=True)
        ST[rows] = jnp.where(lane < 64, ssq, sdot)
        stats.append(remote("stat", ST.at[rows], STR.at[rows], sibling))
        send(stats[i])
    gain_part = jnp.zeros((1, COLS), F32)
    for i in range(4):
        rows = pl.ds(i * 128, 128)
        stats[i].wait_recv()
        both = ST[rows] + STR[rows]
        ssq = both[:, 0:1] * (1.0 / (2 * COLS))
        sdot = both[:, 64:65] * (1.0 / (2 * COLS))
        inverse = lax.rsqrt(ssq + 1e-06)
        normed = ACC[rows] * inverse
        cot = COT[rows].astype(F32)
        scaled = cot * gain
        GK[rows] = (inverse * (scaled - normed * (inverse * sdot))).astype(BF16)
        gain_part += jnp.sum(cot * normed, axis=0, keepdims=True)
    GX[x] = gain_part

    other = 1 - p
    half = [pl.ds(CR + k * AH, AH) for k in range(2)]

    def partial(pos):
        G[zo(pos)] = lax.dot_general(
            X[zo(pos)], GK[...], (((0,), (0,)), ((), ())), preferred_element_type=F32
        ).astype(BF16).reshape(2, ROWS, COLS)

    def y_wide(pos):
        for k in range(2):
            cp["yw", pos, k] = remote("ry", G.at[zo(pos), other, crow[k]], YR.at[pos, crow[k]], dev(dy=1 if k == 0 else 3))
            send(cp["yw", pos, k])

    def x_far(pos):
        for way in range(2):
            rows = half_of(x + 2, way)
            cp["x1", pos, way] = remote("rx", G.at[zo(pos), :, rows], XR.at[pos, way, 0], dev(dx=1 if way == 0 else 3))
            send(cp["x1", pos, way])

    def x_near(pos):
        for way in range(2):
            step = 1 if way == 0 else 3
            rows = half_of(x + step, 1 - way)
            cp["x2", pos, way] = remote("rx", G.at[zo(pos), :, rows], XR.at[pos, way, 1], dev(dx=step))
            send(cp["x2", pos, way])

    def x_second(pos, way):
        at = zo(pos)
        step = 1 if way == 0 else 3
        rows = half_of(x + step, way)
        got("x1", pos, way)
        for parity in range(2):
            G[at, parity, rows] = (G[at, parity, rows].astype(F32) + XR[pos, way, 0, parity].astype(F32)).astype(BF16)
        cp["x3", pos, way] = remote("rx", G.at[at, :, rows], XR.at[pos, way, 2], dev(dx=step))
        send(cp["x3", pos, way])

    def x_third(pos):
        at = zo(pos)
        for way in range(2):
            got("x2", pos, way)
            got("x3", pos, way)
        for k in range(2):
            for parity in range(2):
                total = G[at, parity, arow[k]].astype(F32) + XR[pos, k, 2, parity].astype(F32)
                total = total + XR[pos, 1 - k, 1, parity].astype(F32)
                G[at, parity, arow[k]] = total.astype(BF16)
        for k in range(2):
            cp["yn", pos, k] = remote("ry", G.at[at, other, arow[k]], YR.at[pos, half[k]], dev(dy=1 if k == 0 else 3))
            send(cp["yn", pos, k])

    def owner(sig, d):
        return 0 if d == 0 else 7 if d == 4 else POS[sig * d]

    def first_half(sig):
        return 0 if sig == 1 else 1

    def z_sum(sig, d, k, name):
        pos, at, way = owner(sig, d), zo(owner(sig, d)), 0 if sig == 1 else 1
        rows, buf = (crow[k], crow[k]) if name == "w" else (arow[k], half[k])
        got("y" + name, pos, k)
        total = G[at, p, rows].astype(F32) + YR[pos, buf].astype(F32)
        if d < 3 or (d == 3 and k == first_half(sig)):
            got("z" + name, sig, d, k)
            total = total + ZR[way, d, buf].astype(F32)
        G[at, p, rows] = total.astype(BF16)
        cp["z" + name, sig, d - 1, k] = remote("rz", G.at[at, p, rows], ZR.at[way, d - 1, buf], dev(dz=sig % 8))
        send(cp["z" + name, sig, d - 1, k])

    gtc = {}

    def gt(pos):
        at = zo(pos)
        weight = W[at].reshape(PAIR, COLS)
        TS[pos] = lax.dot_general(
            GK[sib_toks], weight, (((1,), (1,)), ((), ())), preferred_element_type=F32
        ).astype(BF16)
        copy = remote("gt", TS.at[pos], TR.at[pos], sibling)
        gtc[pos] = copy
        send(copy)
        TM[pos] = lax.dot_general(
            GK[my_toks], weight, (((1,), (1,)), ((), ())), preferred_element_type=F32
        )

    def gt_end(pos):
        gtc[pos].wait_recv()
        gt_ref[:, pl.ds(aligned(zo(pos) * PAIR, 128), PAIR)] = (TM[pos] + TR[pos].astype(F32)).astype(BF16)

    def gain_send(name, buf, mine, hops):
        for hop in hops:
            cp["gain" + name, hop] = remote("gg", buf.at[mine], buf.at[mine], dev(**{"d" + name: hop}))
            send(cp["gain" + name, hop])

    def gain_sum(name, buf, hops):
        for hop in hops:
            got("gain" + name, hop)
        total = buf[0]
        for i in range(1, len(hops) + 1):
            total = total + buf[i]
        return total

    def gain_step(i):
        if i == 0:
            gain_send("x", GX, x, (1, 3, 2))
        elif i == 1:
            GY[y] = gain_sum("x", GX, (1, 3, 2))
            gain_send("y", GY, y, (1, 3, 2))
        elif i == 2:
            GZ[z] = gain_sum("y", GY, (1, 3, 2))
            gain_send("z", GZ, z, (1, 7, 2, 6, 3, 5, 4))
        else:
            GB[...] = gain_sum("z", GZ, (1, 7, 2, 6, 3, 5, 4)) * (1.0 / DEVICES)

    gain_step(0)
    partial(7)
    x_far(7)
    y_wide(7)
    partial(5)
    x_near(7)
    partial(6)
    x_far(5)
    partial(3)
    x_near(5)
    y_wide(5)
    partial(4)
    x_second(7, 0)
    x_second(7, 1)
    partial(1)
    partial(2)
    x_far(6)
    partial(0)
    x_near(6)
    z_sum(-1, 4, 1, 'w')
    y_wide(6)
    z_sum(1, 4, 0, 'w')
    x_far(3)
    x_second(5, 1)
    x_second(5, 0)
    gt(7)
    x_third(7)
    gt(5)
    x_near(3)
    y_wide(3)
    z_sum(1, 3, 1, 'w')
    x_second(6, 0)
    x_second(6, 1)
    gt(6)
    x_far(4)
    x_second(3, 0)
    x_second(3, 1)
    gt(3)
    z_sum(-1, 3, 1, 'w')
    gain_step(1)
    z_sum(1, 4, 0, 'n')
    z_sum(-1, 4, 1, 'n')
    y_wide(4)
    x_near(4)
    z_sum(1, 3, 0, 'w')
    z_sum(-1, 3, 0, 'w')
    x_third(5)
    x_far(1)
    x_third(6)
    x_near(1)
    x_second(4, 0)
    z_sum(1, 2, 1, 'w')
    x_second(4, 1)
    x_third(3)
    x_far(2)
    y_wide(1)
    x_near(2)
    x_second(1, 1)
    z_sum(-1, 2, 1, 'w')
    z_sum(1, 2, 0, 'w')
    z_sum(1, 3, 1, 'n')
    z_sum(1, 3, 0, 'n')
    x_second(1, 0)
    z_sum(-1, 3, 1, 'n')
    z_sum(-1, 3, 0, 'n')
    x_third(4)
    x_far(0)
    gain_step(2)
    x_near(0)
    z_sum(-1, 2, 0, 'w')
    y_wide(2)
    x_second(2, 0)
    x_second(2, 1)
    x_third(1)
    z_sum(1, 1, 1, 'w')
    x_second(0, 0)
    x_second(0, 1)
    y_wide(0)
    z_sum(1, 1, 0, 'w')
    z_sum(-1, 2, 1, 'n')
    z_sum(1, 2, 1, 'n')
    z_sum(-1, 2, 0, 'n')
    z_sum(1, 2, 0, 'n')
    x_third(2)
    z_sum(-1, 1, 1, 'w')
    x_third(0)
    z_sum(-1, 1, 0, 'w')
    z_sum(-1, 1, 0, 'n')
    z_sum(-1, 1, 1, 'n')
    z_sum(1, 1, 1, 'n')
    z_sum(1, 1, 0, 'n')

    others = [(1, 0), (3, 0), (2, 0), (0, 1), (1, 1), (3, 1), (2, 1)]

    def wide_block(dx, dh):
        return pl.ds(aligned((h + dh) % 2 * CH, CH), CH), pl.ds(aligned((x + dx + 4) % 4 * 128, 128), 128)

    def narrow_block(dx, dh):
        return pl.ds(aligned(CR + (x + dx + 4) % 4 * AQ + (h + dh) % 2 * AH, AH), AH)

    for sig in (1, -1):
        for k in range(2):
            got("zw", sig, 0, k)
    for k in range(2):
        got("yw", 0, k)
    mine = YR[0, 0:CR].astype(F32) + G[z, p, 0:CR].astype(F32)
    mine = mine + ZR[0, 0, 0:CR].astype(F32) + ZR[1, 0, 0:CR].astype(F32)
    SF[...] = mine
    SB[...] = mine.astype(BF16)
    for i, (dx, dh) in enumerate(others):
        cp["ax", i] = remote("ax", SB.at[wide_block(dx, dh)], AX.at[i], dev(dx=dx, dy=2 * dh))
        send(cp["ax", i])
    for sig in (1, -1):
        for k in range(2):
            got("zn", sig, 0, k)
    for k in range(2):
        got("yn", 0, k)
    last = G[z, p, axq].astype(F32) + YR[0, CR:].astype(F32)
    NB[...] = last + ZR[0, 0, CR:].astype(F32) + ZR[1, 0, CR:].astype(F32)
    ah = remote("ah", NB.at[pl.ds(aligned((1 - h) * AH, AH), AH)], NR, dev(dy=2))
    send(ah)
    for q in (4, 1, 2, 0):
        gt(q)
    for q in (7, 5, 6, 3):
        gt_end(q)
    def hand_out(name, ref):
        for i, (dx, dh) in enumerate(others):
            cp[name, i] = remote("af", ref, ref, dev(dx=dx, dy=2 * dh))
            send(cp[name, i])
        far.append(remote("ac", ref, ref, sibling))
        send(far[-1])

    far = []
    ah.wait_recv()
    FO[c, narrow_block(0, 0)] = ((NB[pl.ds(aligned(h * AH, AH), AH)] + NR[...]) * (1.0 / DEVICES)).astype(BF16)
    hand_out("narrow", FO.at[c, narrow_block(0, 0)])
    total = SF[wide_block(0, 0)]
    for i in range(len(others)):
        got("ax", i)
        total = total + AX[i].astype(F32)
    FO[(c,) + wide_block(0, 0)] = (total * (1.0 / DEVICES)).astype(BF16)
    hand_out("wide", FO.at[(c,) + wide_block(0, 0)])
    gain_step(3)
    gg_out = [local(GB, gg_ref.at[:, my_cols])]
    gg_far = remote("go", GB, gg_ref.at[:, my_cols], sibling)
    send(gg_far)

    for q in (4, 1, 2, 0):
        gt_end(q)
    for i, (dx, dh) in enumerate(others):
        for name, ref in (("narrow", FO.at[c, narrow_block(-dx, dh)]), ("wide", FO.at[(c,) + wide_block(-dx, dh)])):
            got(name, i)
            far.append(remote("ac", ref, ref, sibling))
            send(far[-1])
    for copy in far:
        copy.wait_recv()
    gw_ref[...] = FO[...]
    gg_far.wait_recv()
    for copy in gg_out:
        copy.wait()
    for copy in open_sends:
        copy.wait_send()


def finish(gt_in, gw_in, gg_in, gt_ref, gw_ref, gg_ref, wide, sem):
    copies = []
    for i in range(4):
        rows = pl.ds(i * TOK // 4, TOK // 4)
        copies.append(pltpu.make_async_copy(gt_in.at[rows], gt_ref.at[rows], sem.at[i]))
    copies.append(pltpu.make_async_copy(gg_in, gg_ref, sem.at[4]))
    for copy in copies:
        copy.start()
    for i in range(2):
        rows = pl.ds(i * ROWS // 2, ROWS // 2)
        for half in range(2):
            wide[rows, half * COLS : (half + 1) * COLS] = gw_in[half, rows].astype(F32)
        copies.append(pltpu.make_async_copy(wide.at[rows], gw_ref.at[rows], sem.at[5 + i]))
        copies[-1].start()
    for copy in copies:
        copy.wait()


SEMS = {"gz": 30, "gy": 32, "gx": 32, "swap": 9, "stat": 4, "rx": 48, "ry": 32, "rz": 28, "gt": 8, "gg": 13,
        "go": 1, "ax": 7, "ah": 1, "af": 14, "ac": 16}
GROUPS = tuple(SEMS)


def per_device(tokens, key_weight, key_gain, key_cotangent):
    anywhere = pl.BlockSpec(memory_space=pl.ANY)
    vmem = pl.BlockSpec(memory_space=pltpu.VMEM)
    sems = []
    for group in GROUPS:
        sems += [pltpu.SemaphoreType.DMA((SEMS[group],))] * 2
    V = pltpu.VMEM
    grad_tokens, grad_weight, grad_gain = pl.pallas_call(
        kernel,
        out_shape=(
            pltpu.VMEM((TOK, 5120), BF16),
            pltpu.VMEM((2, ROWS, COLS), BF16),
            pltpu.VMEM((1, 1024), F32),
        ),
        in_specs=[anywhere, anywhere, vmem, anywhere],
        out_specs=(vmem, vmem, vmem),
        scratch_shapes=[
            V((8, 2, ROWS, COLS), BF16),
            V((8, 2 * TOK, PAIR), BF16),
            V((2 * TOK, COLS), BF16),
            V((2 * TOK, COLS), F32),
            V((2 * TOK, COLS), BF16),
            V((2 * TOK, 128), F32),
            V((2 * TOK, 128), F32),
            V((8, 2, ROWS, COLS), BF16),
            V((8, 2, 3, 2, AH, COLS), BF16),
            V((8, CR + AQ, COLS), BF16),
            V((2, 4, CR + AQ, COLS), BF16),
            V((CR, COLS), BF16),
            V((CR, COLS), F32),
            V((7, CH, 128), BF16),
            V((AQ, COLS), F32),
            V((AH, COLS), F32),
            V((2, ROWS, COLS), BF16),
            V((8, TOK, PAIR), BF16),
            V((8, TOK, PAIR), BF16),
            V((8, TOK, PAIR), F32),
            V((1, COLS), F32),
            V((4, 1, COLS), F32),
            V((4, 1, COLS), F32),
            V((8, 1, COLS), F32),
            pltpu.SemaphoreType.DMA((24,)),
            *sems,
        ],
        compiler_params=pltpu.CompilerParams(
            collective_id=0, has_side_effects=True, vmem_limit_bytes=58 * 2**20
        ),
        name="key_projection_backward",
    )(tokens, key_weight, key_gain.reshape(1, 1024), key_cotangent)
    grad_tokens, grad_weight, grad_gain = pl.pallas_call(
        finish,
        out_shape=(
            jax.ShapeDtypeStruct((TOK, 5120), BF16),
            jax.ShapeDtypeStruct((ROWS, 1024), F32),
            jax.ShapeDtypeStruct((1, 1024), F32),
        ),
        in_specs=[vmem, vmem, vmem],
        out_specs=(anywhere, anywhere, anywhere),
        scratch_shapes=[pltpu.VMEM((ROWS, 1024), F32), pltpu.SemaphoreType.DMA((7,))],
        compiler_params=pltpu.CompilerParams(vmem_limit_bytes=16 * 2**20),
        name="write_results",
    )(grad_tokens, grad_weight, grad_gain)
    return grad_tokens, grad_weight, grad_gain.reshape(1024)


def solution(mesh):
    return jax.shard_map(
        per_device,
        mesh=mesh,
        in_specs=(P(("rep", "shard"), None), P("shard", None), P(), P(("rep", "shard"), None)),
        out_specs=(P(("rep", "shard"), None), P("shard", None), P()),
        check_vma=False,
    )
```

```python
import jax
import jax.numpy as jnp
from jax import lax
from jax.experimental import pallas as pl
from jax.experimental.pallas import tpu as pltpu
from jax.sharding import PartitionSpec as P

MESH = pl.DeviceIdType.MESH
F32 = jnp.float32
BF16 = jnp.bfloat16

ROWS = 320
PAIR = 640
COLS = 512
TOK = 256
CR = 192
CH = 96
AQ = 32
AH = 16
OFFS = (0, 1, -1, 2, -2, 3, -3, 4)
POS = {off: i for i, off in enumerate(OFFS)}
DEVICES = 256


def aligned(value, to):
    return pl.multiple_of(value, to)


def kernel(
    tok_ref, w_ref, gain_ref, cot_ref,
    gt_ref, gw_ref, gg_ref,
    W, X, COT, ACC, GK, ST, STR,
    G, XR, YR, ZR, SB, SF, AX, NB, NR, FO,
    TS, TR, TM, GB, GX, GY, GZ,
    lsem, *sems,
):
    rep, shard = lax.axis_index("rep"), lax.axis_index("shard")
    x, h, c = rep // 4, (rep // 2) % 2, rep % 2
    z, p = shard // 2, shard % 2
    y = 2 * h + p

    def dev(dx=0, dy=0, dz=0, core=None):
        xx, yy, zz = (x + dx + 4) % 4, (y + dy) % 4, (z + dz) % 8
        cc = c if core is None else core
        return {"rep": xx * 4 + (yy // 2) * 2 + cc, "shard": zz * 2 + yy % 2}

    sibling = dev(core=1 - c)
    def zo(pos):
        return (z + OFFS[pos] + 8) % 8

    counters = {}
    open_sends = []

    def remote(group, src, dst, to):
        ss, rs = sems[2 * GROUPS.index(group)], sems[2 * GROUPS.index(group) + 1]
        i = counters.get(group, 0)
        counters[group] = i + 1
        assert i < SEMS[group], group
        return pltpu.make_async_remote_copy(
            src_ref=src, dst_ref=dst, send_sem=ss.at[i], recv_sem=rs.at[i],
            device_id=to, device_id_type=MESH,
        )

    def send(copy):
        copy.start()
        open_sends.append(copy)

    lcount = [0]

    def local(src, dst):
        i = lcount[0]
        lcount[0] += 1
        copy = pltpu.make_async_copy(src, dst, lsem.at[i])
        copy.start()
        return copy

    my_cols = pl.ds(aligned(c * COLS, COLS), COLS)
    sib_cols = pl.ds(aligned((1 - c) * COLS, COLS), COLS)
    my_toks = pl.ds(aligned(c * TOK, TOK), TOK)
    sib_toks = pl.ds(aligned((1 - c) * TOK, TOK), TOK)

    w_load = local(w_ref.at[:, my_cols], W.at[z, p])
    loads = [local(cot_ref.at[:, my_cols], COT.at[my_toks])]
    for q in range(8):
        loads.append(local(tok_ref.at[:, pl.ds(q * PAIR, PAIR)], X.at[q, my_toks]))

    partners = [dev(dx=i) for i in range(1, 4)] + [dev(dy=i) for i in range(1, 4)]
    partners += [dev(dz=i) for i in range(1, 8)] + [dev(dx=i, dy=2) for i in range(1, 4)] + [sibling]
    barrier = pltpu.get_barrier_semaphore()
    for to in partners:
        pl.semaphore_signal(barrier, inc=1, device_id=to, device_id_type=MESH)
    pl.semaphore_wait(barrier, len(partners))

    crow = [pl.ds(k * CH, CH) for k in range(2)]
    arow = [pl.ds(aligned(CR + x * AQ + k * AH, AH), AH) for k in range(2)]
    axq = pl.ds(aligned(CR + x * AQ, AQ), AQ)
    cp, seen = {}, set()

    def at_step(sig, d):
        return 0 if d == 0 else 7 if d == 4 else POS[-sig * d]

    def zc(sig, d, k):
        ref = W.at[zo(at_step(sig, d - 1)), p, crow[k]]
        cp["zc", sig, d, k] = remote("gz", ref, ref, dev(dz=sig % 8))
        send(cp["zc", sig, d, k])

    def za(sig, d):
        rows = axq if d < 4 else arow[0 if sig == 1 else 1]
        ref = W.at[zo(at_step(sig, d - 1)), p, rows]
        cp["za", sig, d] = remote("gz", ref, ref, dev(dz=sig % 8))
        send(cp["za", sig, d])

    def yc(pos, k):
        ref = W.at[zo(pos), p, crow[k]]
        cp["yc", pos, k] = remote("gy", ref, ref, dev(dy=1 if k == 0 else 3))
        send(cp["yc", pos, k])

    def ya(pos, k):
        ref = W.at[zo(pos), p, arow[k]]
        cp["ya", pos, k] = remote("gy", ref, ref, dev(dy=1 if k == 0 else 3))
        send(cp["ya", pos, k])

    def half_of(quarter, k):
        return pl.ds(aligned(CR + (quarter % 4) * AQ + k * AH, AH), AH)

    def xs(pos):
        for k in range(2):
            got("ya", pos, k)
        ref = W.at[zo(pos), pl.ds(1 - p, 1), axq] if pos == 0 else W.at[zo(pos), :, axq]
        for way in range(2):
            cp["xs", pos, way] = remote("gx", ref, ref, dev(dx=1 if way == 0 else 3))
            send(cp["xs", pos, way])

    def xr(pos, way):
        got("xs", pos, way)
        rows = half_of(x + (3 if way == 0 else 1), way)
        ref = W.at[zo(pos), pl.ds(1 - p, 1), rows] if pos == 0 else W.at[zo(pos), :, rows]
        cp["xr", pos, way] = remote("gx", ref, ref, dev(dx=1 if way == 0 else 3))
        send(cp["xr", pos, way])

    def got(*key):
        if key not in seen:
            seen.add(key)
            cp[key].wait_recv()

    def project(pos, first=False):
        at = zo(pos)

        @pl.loop(0, 2)
        def _(i):
            rows = pl.ds(aligned(i * TOK, TOK), TOK)
            part = jnp.dot(X[at, rows], W[at].reshape(PAIR, COLS), preferred_element_type=F32)
            if first:
                ACC[rows] = part
            else:
                ACC[rows] += part

    def positions(d):
        return [0] if d == 0 else [7] if d == 4 else [POS[d], POS[-d]]

    def a_step(d):
        for sig in (1, -1):
            got("za", sig, d)
            if d < 4:
                za(sig, d + 1)
                for k in range(2):
                    ya(at_step(sig, d), k)
            else:
                ya(7, 0 if sig == 1 else 1)

    def ax_step(d):
        for pos in positions(d):
            xs(pos)

    def xr_step(d):
        for pos in positions(d):
            xr(pos, 0)
            xr(pos, 1)

    def c_step(d, j):
        for sig in (1, -1):
            k = j if sig == 1 else 1 - j
            got("zc", sig, d, k)
            if d < 3 or (d == 3 and j == 0):
                zc(sig, d + 1, k)
            yc(at_step(sig, d), k)

    def finish(d):
        for pos in positions(d):
            for k in range(2):
                got("yc", pos, k)
            for way in range(2):
                got("xs", pos, way)
                got("xr", pos, way)
            project(pos, first=pos == 0)

    w_load.wait()
    za(1, 1)
    za(-1, 1)
    ya(0, 0)
    ya(0, 1)
    zc(1, 1, 0)
    zc(-1, 1, 1)
    yc(0, 0)
    yc(0, 1)
    swaps = [remote("swap", cot_ref.at[:, sib_cols], COT.at[my_toks], sibling)]
    for q in range(8):
        swaps.append(remote("swap", tok_ref.at[:, pl.ds(q * PAIR, PAIR)], X.at[q, my_toks], sibling))
    for copy in swaps:
        send(copy)
    a_step(1)
    zc(1, 1, 1)
    zc(-1, 1, 0)
    ax_step(0)
    c_step(1, 0)
    a_step(2)
    ax_step(1)
    c_step(1, 1)
    a_step(3)
    c_step(2, 0)
    ax_step(2)
    xr_step(0)
    c_step(2, 1)
    a_step(4)
    xr_step(1)
    ax_step(3)
    ax_step(4)
    c_step(3, 0)
    xr_step(2)
    for copy in loads:
        copy.wait()
    for copy in swaps:
        copy.wait_recv()
    finish(0)
    c_step(3, 1)
    xr_step(3)
    c_step(4, 0)
    xr_step(4)
    finish(1)
    finish(2)
    finish(3)
    finish(4)

    gain = gain_ref[0:1, my_cols]

    lane = lax.broadcasted_iota(jnp.int32, (128, 128), 1)
    stats = []
    for i in range(4):
        rows = pl.ds(i * 128, 128)
        proj = ACC[rows]
        scaled = COT[rows].astype(F32) * gain
        ssq = jnp.sum(proj * proj, axis=1, keepdims=True)
        sdot = jnp.sum(scaled * proj, axis=1, keepdims=True)
        ST[rows] = jnp.where(lane < 64, ssq, sdot)
        stats.append(remote("stat", ST.at[rows], STR.at[rows], sibling))
        send(stats[i])
    gain_part = jnp.zeros((1, COLS), F32)
    for i in range(4):
        rows = pl.ds(i * 128, 128)
        stats[i].wait_recv()
        both = ST[rows] + STR[rows]
        ssq = both[:, 0:1] * (1.0 / (2 * COLS))
        sdot = both[:, 64:65] * (1.0 / (2 * COLS))
        inverse = lax.rsqrt(ssq + 1e-06)
        normed = ACC[rows] * inverse
        cot = COT[rows].astype(F32)
        scaled = cot * gain
        GK[rows] = (inverse * (scaled - normed * (inverse * sdot))).astype(BF16)
        gain_part += jnp.sum(cot * normed, axis=0, keepdims=True)
    GX[x] = gain_part

    other = 1 - p
    half = [pl.ds(CR + k * AH, AH) for k in range(2)]

    def partial(pos):
        G[zo(pos)] = lax.dot_general(
            X[zo(pos)], GK[...], (((0,), (0,)), ((), ())), preferred_element_type=F32
        ).astype(BF16).reshape(2, ROWS, COLS)

    def y_wide(pos):
        for k in range(2):
            cp["yw", pos, k] = remote("ry", G.at[zo(pos), other, crow[k]], YR.at[pos, crow[k]], dev(dy=1 if k == 0 else 3))
            send(cp["yw", pos, k])

    def x_far(pos):
        for way in range(2):
            rows = half_of(x + 2, way)
            cp["x1", pos, way] = remote("rx", G.at[zo(pos), :, rows], XR.at[pos, way, 0], dev(dx=1 if way == 0 else 3))
            send(cp["x1", pos, way])

    def x_near(pos):
        for way in range(2):
            step = 1 if way == 0 else 3
            rows = half_of(x + step, 1 - way)
            cp["x2", pos, way] = remote("rx", G.at[zo(pos), :, rows], XR.at[pos, way, 1], dev(dx=step))
            send(cp["x2", pos, way])

    def x_second(pos, way):
        at = zo(pos)
        step = 1 if way == 0 else 3
        rows = half_of(x + step, way)
        got("x1", pos, way)
        for parity in range(2):
            G[at, parity, rows] = (G[at, parity, rows].astype(F32) + XR[pos, way, 0, parity].astype(F32)).astype(BF16)
        cp["x3", pos, way] = remote("rx", G.at[at, :, rows], XR.at[pos, way, 2], dev(dx=step))
        send(cp["x3", pos, way])

    def x_third(pos):
        at = zo(pos)
        for way in range(2):
            got("x2", pos, way)
            got("x3", pos, way)
        for k in range(2):
            for parity in range(2):
                total = G[at, parity, arow[k]].astype(F32) + XR[pos, k, 2, parity].astype(F32)
                total = total + XR[pos, 1 - k, 1, parity].astype(F32)
                G[at, parity, arow[k]] = total.astype(BF16)
        for k in range(2):
            cp["yn", pos, k] = remote("ry", G.at[at, other, arow[k]], YR.at[pos, half[k]], dev(dy=1 if k == 0 else 3))
            send(cp["yn", pos, k])

    def owner(sig, d):
        return 0 if d == 0 else 7 if d == 4 else POS[sig * d]

    def first_half(sig):
        return 0 if sig == 1 else 1

    def z_sum(sig, d, k, name):
        pos, at, way = owner(sig, d), zo(owner(sig, d)), 0 if sig == 1 else 1
        rows, buf = (crow[k], crow[k]) if name == "w" else (arow[k], half[k])
        got("y" + name, pos, k)
        total = G[at, p, rows].astype(F32) + YR[pos, buf].astype(F32)
        if d < 3 or (d == 3 and k == first_half(sig)):
            got("z" + name, sig, d, k)
            total = total + ZR[way, d, buf].astype(F32)
        G[at, p, rows] = total.astype(BF16)
        cp["z" + name, sig, d - 1, k] = remote("rz", G.at[at, p, rows], ZR.at[way, d - 1, buf], dev(dz=sig % 8))
        send(cp["z" + name, sig, d - 1, k])

    gtc = {}

    def gt(pos):
        at = zo(pos)
        weight = W[at].reshape(PAIR, COLS)
        TS[pos] = lax.dot_general(
            GK[sib_toks], weight, (((1,), (1,)), ((), ())), preferred_element_type=F32
        ).astype(BF16)
        copy = remote("gt", TS.at[pos], TR.at[pos], sibling)
        gtc[pos] = copy
        send(copy)
        TM[pos] = lax.dot_general(
            GK[my_toks], weight, (((1,), (1,)), ((), ())), preferred_element_type=F32
        )

    def gt_end(pos):
        gtc[pos].wait_recv()
        gt_ref[:, pl.ds(aligned(zo(pos) * PAIR, 128), PAIR)] = (TM[pos] + TR[pos].astype(F32)).astype(BF16)

    def gain_send(name, buf, mine, hops):
        for hop in hops:
            cp["gain" + name, hop] = remote("gg", buf.at[mine], buf.at[mine], dev(**{"d" + name: hop}))
            send(cp["gain" + name, hop])

    def gain_sum(name, buf, hops):
        for hop in hops:
            got("gain" + name, hop)
        total = buf[0]
        for i in range(1, len(hops) + 1):
            total = total + buf[i]
        return total

    def gain_step(i):
        if i == 0:
            gain_send("x", GX, x, (1, 3, 2))
        elif i == 1:
            GY[y] = gain_sum("x", GX, (1, 3, 2))
            gain_send("y", GY, y, (1, 3, 2))
        elif i == 2:
            GZ[z] = gain_sum("y", GY, (1, 3, 2))
            gain_send("z", GZ, z, (1, 7, 2, 6, 3, 5, 4))
        else:
            GB[...] = gain_sum("z", GZ, (1, 7, 2, 6, 3, 5, 4)) * (1.0 / DEVICES)

    gain_step(0)
    partial(7)
    x_far(7)
    y_wide(7)
    partial(5)
    x_near(7)
    partial(6)
    x_far(5)
    partial(3)
    x_near(5)
    y_wide(5)
    partial(4)
    x_second(7, 0)
    x_second(7, 1)
    partial(1)
    partial(2)
    x_far(6)
    partial(0)
    x_near(6)
    z_sum(-1, 4, 1, 'w')
    y_wide(6)
    z_sum(1, 4, 0, 'w')
    x_far(3)
    x_second(5, 1)
    x_second(5, 0)
    gt(7)
    x_third(7)
    gt(5)
    x_near(3)
    y_wide(3)
    z_sum(1, 3, 1, 'w')
    x_second(6, 0)
    x_second(6, 1)
    gt(6)
    x_far(4)
    x_second(3, 0)
    x_second(3, 1)
    gt(3)
    z_sum(-1, 3, 1, 'w')
    gain_step(1)
    z_sum(1, 4, 0, 'n')
    z_sum(-1, 4, 1, 'n')
    y_wide(4)
    x_near(4)
    z_sum(1, 3, 0, 'w')
    z_sum(-1, 3, 0, 'w')
    x_third(5)
    x_far(1)
    x_third(6)
    x_near(1)
    x_second(4, 0)
    z_sum(1, 2, 1, 'w')
    x_second(4, 1)
    x_third(3)
    x_far(2)
    y_wide(1)
    x_near(2)
    x_second(1, 1)
    z_sum(-1, 2, 1, 'w')
    z_sum(1, 2, 0, 'w')
    z_sum(1, 3, 1, 'n')
    z_sum(1, 3, 0, 'n')
    x_second(1, 0)
    z_sum(-1, 3, 1, 'n')
    z_sum(-1, 3, 0, 'n')
    x_third(4)
    x_far(0)
    gain_step(2)
    x_near(0)
    z_sum(-1, 2, 0, 'w')
    y_wide(2)
    x_second(2, 0)
    x_second(2, 1)
    x_third(1)
    z_sum(1, 1, 1, 'w')
    x_second(0, 0)
    x_second(0, 1)
    y_wide(0)
    z_sum(1, 1, 0, 'w')
    z_sum(-1, 2, 1, 'n')
    z_sum(1, 2, 1, 'n')
    z_sum(-1, 2, 0, 'n')
    z_sum(1, 2, 0, 'n')
    x_third(2)
    z_sum(-1, 1, 1, 'w')
    x_third(0)
    z_sum(-1, 1, 0, 'w')
    z_sum(-1, 1, 0, 'n')
    z_sum(-1, 1, 1, 'n')
    z_sum(1, 1, 1, 'n')
    z_sum(1, 1, 0, 'n')

    others = [(1, 0), (3, 0), (2, 0), (0, 1), (1, 1), (3, 1), (2, 1)]

    def wide_block(dx, dh):
        return pl.ds(aligned((h + dh) % 2 * CH, CH), CH), pl.ds(aligned((x + dx + 4) % 4 * 128, 128), 128)

    def narrow_block(dx, dh):
        return pl.ds(aligned(CR + (x + dx + 4) % 4 * AQ + (h + dh) % 2 * AH, AH), AH)

    for sig in (1, -1):
        for k in range(2):
            got("zw", sig, 0, k)
    for k in range(2):
        got("yw", 0, k)
    mine = YR[0, 0:CR].astype(F32) + G[z, p, 0:CR].astype(F32)
    mine = mine + ZR[0, 0, 0:CR].astype(F32) + ZR[1, 0, 0:CR].astype(F32)
    SF[...] = mine
    SB[...] = mine.astype(BF16)
    for i, (dx, dh) in enumerate(others):
        cp["ax", i] = remote("ax", SB.at[wide_block(dx, dh)], AX.at[i], dev(dx=dx, dy=2 * dh))
        send(cp["ax", i])
    for sig in (1, -1):
        for k in range(2):
            got("zn", sig, 0, k)
    for k in range(2):
        got("yn", 0, k)
    last = G[z, p, axq].astype(F32) + YR[0, CR:].astype(F32)
    NB[...] = last + ZR[0, 0, CR:].astype(F32) + ZR[1, 0, CR:].astype(F32)
    ah = remote("ah", NB.at[pl.ds(aligned((1 - h) * AH, AH), AH)], NR, dev(dy=2))
    send(ah)
    for q in (4, 1, 2, 0):
        gt(q)
    for q in (7, 5, 6, 3):
        gt_end(q)
    def hand_out(name, ref):
        for i, (dx, dh) in enumerate(others):
            cp[name, i] = remote("af", ref, ref, dev(dx=dx, dy=2 * dh))
            send(cp[name, i])
        far.append(remote("ac", ref, ref, sibling))
        send(far[-1])

    far = []
    ah.wait_recv()
    FO[c, narrow_block(0, 0)] = ((NB[pl.ds(aligned(h * AH, AH), AH)] + NR[...]) * (1.0 / DEVICES)).astype(BF16)
    hand_out("narrow", FO.at[c, narrow_block(0, 0)])
    total = SF[wide_block(0, 0)]
    for i in range(len(others)):
        got("ax", i)
        total = total + AX[i].astype(F32)
    FO[(c,) + wide_block(0, 0)] = (total * (1.0 / DEVICES)).astype(BF16)
    hand_out("wide", FO.at[(c,) + wide_block(0, 0)])
    gain_step(3)
    gg_out = [local(GB, gg_ref.at[:, my_cols])]
    gg_far = remote("go", GB, gg_ref.at[:, my_cols], sibling)
    send(gg_far)

    for q in (4, 1, 2, 0):
        gt_end(q)
    for i, (dx, dh) in enumerate(others):
        for name, ref in (("narrow", FO.at[c, narrow_block(-dx, dh)]), ("wide", FO.at[(c,) + wide_block(-dx, dh)])):
            got(name, i)
            far.append(remote("ac", ref, ref, sibling))
            send(far[-1])
    for copy in far:
        copy.wait_recv()
    gw_ref[...] = FO[...]
    gg_far.wait_recv()
    for copy in gg_out:
        copy.wait()
    for copy in open_sends:
        copy.wait_send()


def finish(gt_in, gw_in, gg_in, gt_ref, gw_ref, gg_ref, wide, sem):
    copies = []
    for i in range(4):
        rows = pl.ds(i * TOK // 4, TOK // 4)
        copies.append(pltpu.make_async_copy(gt_in.at[rows], gt_ref.at[rows], sem.at[i]))
    copies.append(pltpu.make_async_copy(gg_in, gg_ref, sem.at[4]))
    for copy in copies:
        copy.start()
    for i in range(2):
        rows = pl.ds(i * ROWS // 2, ROWS // 2)
        for half in range(2):
            wide[rows, half * COLS : (half + 1) * COLS] = gw_in[half, rows].astype(F32)
        copies.append(pltpu.make_async_copy(wide.at[rows], gw_ref.at[rows], sem.at[5 + i]))
        copies[-1].start()
    for copy in copies:
        copy.wait()


SEMS = {"gz": 30, "gy": 32, "gx": 32, "swap": 9, "stat": 4, "rx": 48, "ry": 32, "rz": 28, "gt": 8, "gg": 13,
        "go": 1, "ax": 7, "ah": 1, "af": 14, "ac": 16}
GROUPS = tuple(SEMS)


def per_device(tokens, key_weight, key_gain, key_cotangent):
    anywhere = pl.BlockSpec(memory_space=pl.ANY)
    vmem = pl.BlockSpec(memory_space=pltpu.VMEM)
    sems = []
    for group in GROUPS:
        sems += [pltpu.SemaphoreType.DMA((SEMS[group],))] * 2
    V = pltpu.VMEM
    grad_tokens, grad_weight, grad_gain = pl.pallas_call(
        kernel,
        out_shape=(
            pltpu.VMEM((TOK, 5120), BF16),
            pltpu.VMEM((2, ROWS, COLS), BF16),
            pltpu.VMEM((1, 1024), F32),
        ),
        in_specs=[anywhere, anywhere, vmem, anywhere],
        out_specs=(vmem, vmem, vmem),
        scratch_shapes=[
            V((8, 2, ROWS, COLS), BF16),
            V((8, 2 * TOK, PAIR), BF16),
            V((2 * TOK, COLS), BF16),
            V((2 * TOK, COLS), F32),
            V((2 * TOK, COLS), BF16),
            V((2 * TOK, 128), F32),
            V((2 * TOK, 128), F32),
            V((8, 2, ROWS, COLS), BF16),
            V((8, 2, 3, 2, AH, COLS), BF16),
            V((8, CR + AQ, COLS), BF16),
            V((2, 4, CR + AQ, COLS), BF16),
            V((CR, COLS), BF16),
            V((CR, COLS), F32),
            V((7, CH, 128), BF16),
            V((AQ, COLS), F32),
            V((AH, COLS), F32),
            V((2, ROWS, COLS), BF16),
            V((8, TOK, PAIR), BF16),
            V((8, TOK, PAIR), BF16),
            V((8, TOK, PAIR), F32),
            V((1, COLS), F32),
            V((4, 1, COLS), F32),
            V((4, 1, COLS), F32),
            V((8, 1, COLS), F32),
            pltpu.SemaphoreType.DMA((24,)),
            *sems,
        ],
        compiler_params=pltpu.CompilerParams(
            collective_id=0, has_side_effects=True, vmem_limit_bytes=58 * 2**20
        ),
        name="key_projection_backward",
    )(tokens, key_weight, key_gain.reshape(1, 1024), key_cotangent)
    grad_tokens, grad_weight, grad_gain = pl.pallas_call(
        finish,
        out_shape=(
            jax.ShapeDtypeStruct((TOK, 5120), BF16),
            jax.ShapeDtypeStruct((ROWS, 1024), F32),
            jax.ShapeDtypeStruct((1, 1024), F32),
        ),
        in_specs=[vmem, vmem, vmem],
        out_specs=(anywhere, anywhere, anywhere),
        scratch_shapes=[pltpu.VMEM((ROWS, 1024), F32), pltpu.SemaphoreType.DMA((7,))],
        compiler_params=pltpu.CompilerParams(vmem_limit_bytes=16 * 2**20),
        name="write_results",
    )(grad_tokens, grad_weight, grad_gain)
    return grad_tokens, grad_weight, grad_gain.reshape(1024)


def solution(mesh):
    return jax.shard_map(
        per_device,
        mesh=mesh,
        in_specs=(P(("rep", "shard"), None), P("shard", None), P(), P(("rep", "shard"), None)),
        out_specs=(P(("rep", "shard"), None), P("shard", None), P()),
        check_vma=False,
    )
```
